32 devices in a mesh: depth: 32 (over z, y, x, core).
Axes of the slice: x: 2, y: 2, z: 4, core: 2. Of those that a mesh axis runs over, the one named last changes fastest.
Arguments:
- initial: bfloat16 [2, 256, 1536], replicated, may hold values from -6 to 6
- weights: bfloat16 [64, 1536, 1536], P('depth'), may hold values from -0.15625 to 0.15625
- biases: float32 [64, 1536], P('depth'), may hold values from -3 to 3
- step_sizes: float32 [64], P('depth'), may hold values from 0.02 to 0.2
Outputs:
- states: bfloat16 [64, 2, 256, 1536], P('depth')
The draws below stay inside these ranges and needn't reach their ends.
All inputs are finite; a program needn't handle non-finite values.
Results may differ from the reference program's by a relative error of at most 0.013.
The reference program's roundings to bfloat16 on the way count: a program that leaves them out, or rounds other values in their place, can miss the bound.
Values may be sent and summed in bfloat16 or wider, within the bound.
No kernel may reach another device: no remote copies, remote signals or barrier semaphores. Data moves between devices by JAX's collectives and lax.ppermute only.
A program may use at most 64 MiB of HBM per device.

```python
import math
import jax
import jax.numpy as jnp
from jax import lax

D = 1536
ROWS = 256
LAY_DEV = 2
INTERVAL = 8
LAYERS = 64
GROUPS = 4
N_DEPTH = 32


def draw_step_sizes(key, part):
    first_key, second_key = jax.random.split(jax.random.fold_in(key, 7))
    first_draw = jax.random.uniform(first_key, (LAYERS,), jnp.float32)
    second_draw = jax.random.uniform(second_key, (LAYERS,), jnp.float32)
    coarse_rate = jnp.exp(math.log(0.02) + first_draw * math.log(2.5))
    other_rate = jnp.exp(math.log(0.12) + second_draw * math.log(0.2 / 0.12))
    layer_parity = jnp.arange(LAYERS) % 2
    return jnp.where(layer_parity == 0, coarse_rate, other_rate).astype(jnp.float32)


def block_scale(key, shape, shards, smallest, high):
    def one(dim, blocks):
        steps = jax.random.uniform(jax.random.fold_in(jax.random.fold_in(key, 6), dim), (blocks,), jnp.float32, smallest / len(shards), high / len(shards))
        return jnp.repeat(jnp.exp(steps), shape[dim] // blocks).reshape((-1,) + (1,) * (len(shape) - dim - 1))

    gain = one(*shards[0])
    for cut in shards[1:]:
        gain = gain * one(*cut)
    return gain


def noise(rng, shape, deviation, most, shards=(), held_as=jnp.bfloat16):
    factor_of = block_scale(rng, shape, shards, -0.22, 0.18) if shards else 1.0
    result = jax.random.normal(rng, shape, jnp.float32) * deviation * factor_of
    return jnp.minimum(jnp.maximum(result, -most), most).astype(held_as)


def setup_inputs(seed: int = 0) -> dict:
    key_of = jax.random.split(jax.random.key(seed), 5)
    initial = noise(key_of[0], (2, ROWS, D), 1.0, 6.0)
    weights = noise(key_of[1], (LAYERS, D, D), D ** -0.5, 0.15625, ((0, 32),))
    biases = noise(key_of[2], (LAYERS, D), 0.5, 3.0, ((0, 32),), jnp.float32)
    step_sizes = draw_step_sizes(jax.random.fold_in(key_of[4], 71), 0)
    return {"initial": initial, "weights": weights, "biases": biases, "step_sizes": step_sizes}


def advance(entering, weights, biases, step_sizes):
    state = entering.astype(jnp.float32)
    outputs = []
    for layer in range(LAY_DEV):
        pre = jnp.dot(state.astype(jnp.bfloat16), weights[layer], preferred_element_type=jnp.float32) + biases[layer]
        state = state + step_sizes[layer] * jnp.tanh(pre)
        outputs.append(state)
    return jnp.stack(outputs)


def reference(initial, weights, biases, step_sizes):
    row_count = 2 * ROWS
    start_state = initial.reshape(row_count, D)
    weight_blocks = weights.reshape(N_DEPTH, LAY_DEV, D, D)
    bias_blocks = biases.reshape(N_DEPTH, LAY_DEV, D)
    step_blocks = step_sizes.reshape(N_DEPTH, LAY_DEV)
    entries = jnp.broadcast_to(start_state, (N_DEPTH, row_count, D))

    def leave(item):
        return advance(item[0], item[1], item[2], item[3])[-1].astype(jnp.bfloat16)

    for relax_pass in range(2):
        exits = lax.map(leave, (entries, weight_blocks, bias_blocks, step_blocks))
        entries = jnp.concatenate([start_state[None], exits[:-1]], axis=0)
    third_exits = lax.map(leave, (entries, weight_blocks, bias_blocks, step_blocks))
    fresh = jnp.concatenate([start_state[None], third_exits[:-1]], axis=0)
    residuals = fresh.astype(jnp.float32) - entries.astype(jnp.float32)
    grouped_entries = entries.reshape(GROUPS, INTERVAL, row_count, D)
    grouped_weights = weight_blocks[:, 0].reshape(GROUPS, INTERVAL, D, D)
    grouped_biases = bias_blocks[:, 0].reshape(GROUPS, INTERVAL, D)
    grouped_steps = (INTERVAL * LAY_DEV * step_blocks[:, 0]).reshape(GROUPS, INTERVAL)
    grouped_residuals = residuals.reshape(GROUPS, INTERVAL, row_count, D)

    def one_block(item):
        base, correction, weight, bias, coarse_step, residual = item
        anchor = base.astype(jnp.float32)
        moved = anchor + correction.astype(jnp.float32)

        def coarse_map(value):
            pre = jnp.dot(value.astype(jnp.bfloat16), weight, preferred_element_type=jnp.float32) + bias
            return value + coarse_step * jnp.tanh(pre)

        return ((coarse_map(moved) - coarse_map(anchor)) + residual).astype(jnp.bfloat16)

    def link(correction, item):
        base, weight, bias, coarse_step, residual = item
        message = lax.map(one_block, (base, correction, weight, bias, coarse_step, residual))
        return message, message

    zero_group = jnp.zeros((INTERVAL, row_count, D), jnp.bfloat16)
    _, messages = lax.scan(link, zero_group, (grouped_entries[:-1], grouped_weights[:-1], grouped_biases[:-1], grouped_steps[:-1], grouped_residuals[1:]))
    corrections = jnp.concatenate([zero_group[None], messages], axis=0).reshape(N_DEPTH, row_count, D)
    corrected = entries.astype(jnp.float32) + corrections.astype(jnp.float32)

    def finish(item):
        return advance(item[0], item[1], item[2], item[3]).astype(jnp.bfloat16)

    states = lax.map(finish, (corrected, weight_blocks, bias_blocks, step_blocks))
    return states.reshape(LAYERS, 2, ROWS, D)
```

```python
import functools

import jax
import jax.numpy as jnp
from jax import lax
from jax.experimental import pallas as pl
from jax.experimental.pallas import tpu as pltpu
from jax.sharding import PartitionSpec as P

LAY_DEV = 2
INTERVAL = 8

CHUNKS = 4
TILE = 512
VMEM_BYTES = 20 << 20
VMEM = pl.BlockSpec(memory_space=pltpu.VMEM)
ANY = pl.BlockSpec(memory_space=pl.ANY)


def held(value):
    return pltpu.with_memory_space_constraint(value, pltpu.VMEM)


def kept(shape, kind):
    return pltpu.VMEM(shape, kind)


def in_hbm(value):
    return pltpu.with_memory_space_constraint(value, pltpu.HBM)


def passed_along(value, pairs):
    return lax.ppermute(value, "depth", pairs)


def tiles(width):
    tile = TILE if width % TILE == 0 else width
    return [slice(low, low + tile) for low in range(0, width, tile)]


def product(state, weight):
    return jnp.dot(state, weight, preferred_element_type=jnp.float32)


def block_layers(entering, w_ref, p_ref, out_ref, t_ref, state, rounded):
    width = w_ref.shape[2]
    for cols in tiles(width):
        bent = jnp.tanh(product(rounded[...], w_ref[0, :, cols]) + p_ref[0:1, cols])
        if t_ref is not None:
            t_ref[:, cols] = bent
        state[:, cols] = entering[:, cols].astype(jnp.float32) + p_ref[2:3, cols] * bent


def second_layer(w_ref, p_ref, out_ref, state, rounded):
    for cols in tiles(w_ref.shape[2]):
        bent = jnp.tanh(product(rounded[...], w_ref[1, :, cols]) + p_ref[1:2, cols])
        out_ref[:, cols] = (state[:, cols] + p_ref[3:4, cols] * bent).astype(jnp.bfloat16)


def opening_kernel(start_ref, w_hbm, b_ref, h_ref, out_ref, w_ref, p_ref, state, rounded, sems):
    width = w_hbm.shape[2]
    copies = []
    for layer in range(2):
        for cols in tiles(width):
            copy = pltpu.make_async_copy(
                w_hbm.at[layer, :, cols], w_ref.at[layer, :, cols], sems.at[len(copies)]
            )
            copy.start()
            copies.append(copy)
    p_ref[0:2, :] = b_ref[...]
    for layer in range(2):
        p_ref[2 + layer : 3 + layer, :] = jnp.full((1, width), h_ref[layer], jnp.float32)
    p_ref[4:8, :] = jnp.zeros((4, width), jnp.float32)
    for index, cols in enumerate(tiles(width)):
        copies[index].wait()
        bent = jnp.tanh(product(start_ref[...], w_ref[0, :, cols]) + p_ref[0:1, cols])
        state[:, cols] = start_ref[:, cols].astype(jnp.float32) + p_ref[2:3, cols] * bent
    rounded[...] = state[...].astype(jnp.bfloat16)
    for index, cols in enumerate(tiles(width)):
        copies[len(tiles(width)) + index].wait()
        bent = jnp.tanh(product(rounded[...], w_ref[1, :, cols]) + p_ref[1:2, cols])
        out_ref[:, cols] = (state[:, cols] + p_ref[3:4, cols] * bent).astype(jnp.bfloat16)


def pass_kernel(keep, start_ref, arrived_ref, w_ref, p_ref, out_ref, *rest):
    if keep:
        t_ref, entering, state, rounded = rest
    else:
        t_ref, (entering, state, rounded) = None, rest
    first = lax.axis_index("depth") == 0
    entering[...] = jnp.where(first, start_ref[...], arrived_ref[...])
    block_layers(entering, w_ref, p_ref, out_ref, t_ref, state, entering)
    rounded[...] = state[...].astype(jnp.bfloat16)
    second_layer(w_ref, p_ref, out_ref, state, rounded)


def correction_of(start_ref, entry_ref, fresh_ref, moved_ref, entry, correction):
    device = lax.axis_index("depth")
    entry[...] = jnp.where(device == 0, start_ref[...], entry_ref[...])
    anchor = entry[...].astype(jnp.float32)
    residual = fresh_ref[...].astype(jnp.float32) - anchor
    total = residual if moved_ref is None else moved_ref[...].astype(jnp.float32) + residual
    total = jnp.where(device < INTERVAL, 0.0, total)
    correction[...] = total.astype(jnp.bfloat16)


def coarse_kernel(group, *refs):
    if group == 1:
        start_ref, entry_ref, fresh_ref, t_ref, w_ref, p_ref, out_ref, entry, correction, rounded = refs
        moved_ref = None
    else:
        (start_ref, entry_ref, fresh_ref, moved_ref, t_ref, w_ref, p_ref, out_ref, entry, correction, rounded) = refs

    @pl.when(lax.axis_index("depth") // INTERVAL == group)
    def _():
        correction_of(start_ref, entry_ref, fresh_ref, moved_ref, entry, correction)
        rounded[...] = (entry[...].astype(jnp.float32) + correction[...].astype(jnp.float32)).astype(jnp.bfloat16)
        for cols in tiles(w_ref.shape[2]):
            bent = jnp.tanh(product(rounded[...], w_ref[0, :, cols]) + p_ref[0:1, cols])
            change = (INTERVAL * LAY_DEV) * p_ref[2:3, cols] * (bent - t_ref[:, cols])
            out_ref[:, cols] = (correction[:, cols].astype(jnp.float32) + change).astype(jnp.bfloat16)


def final_kernel(start_ref, entry_ref, fresh_ref, moved_ref, w_ref, p_ref, out_ref, entry, correction, state, rounded):
    correction_of(start_ref, entry_ref, fresh_ref, moved_ref, entry, correction)
    state[...] = entry[...].astype(jnp.float32) + correction[...].astype(jnp.float32)
    rounded[...] = state[...].astype(jnp.bfloat16)
    for cols in tiles(w_ref.shape[2]):
        bent = jnp.tanh(product(rounded[...], w_ref[0, :, cols]) + p_ref[0:1, cols])
        state[:, cols] = state[:, cols] + p_ref[2:3, cols] * bent
    rounded[...] = state[...].astype(jnp.bfloat16)
    out_ref[0] = rounded[...]
    second_layer(w_ref, p_ref, out_ref.at[1], state, rounded)


def local(initial, weights, biases, step_sizes):
    count = lax.axis_size("depth")
    groups = count // INTERVAL
    width = initial.shape[2]
    start = initial.reshape(-1, width)
    rows = start.shape[0] // CHUNKS
    one_on = [(source, source + 1) for source in range(count - 1)]

    def call(body, outs, scratch, *operands, specs=None, layers=2):
        flops = 2 * rows * width * width * layers
        return pl.pallas_call(
            body,
            out_shape=outs,
            in_specs=specs or [VMEM] * len(operands),
            out_specs=jax.tree.map(lambda _: VMEM, outs),
            scratch_shapes=scratch,
            compiler_params=pltpu.CompilerParams(vmem_limit_bytes=VMEM_BYTES),
            cost_estimate=pl.CostEstimate(flops=flops, bytes_accessed=rows * width * 8, transcendentals=rows * width * layers),
        )(*(operands if specs else [held(operand) for operand in operands]))

    wide = lambda kind: pltpu.VMEM((rows, width), kind)
    narrow = jax.ShapeDtypeStruct((rows, width), jnp.bfloat16)
    starts = [start[chunk * rows : (chunk + 1) * rows] for chunk in range(CHUNKS)]

    parts = len(tiles(width))
    leaving, w, p = call(
        opening_kernel,
        (narrow, kept(weights.shape, jnp.bfloat16), kept((8, width), jnp.float32)),
        [wide(jnp.float32), wide(jnp.bfloat16), pltpu.SemaphoreType.DMA((2 * parts,))],
        starts[0], in_hbm(weights), biases, step_sizes,
        specs=[VMEM, ANY, VMEM, pl.BlockSpec(memory_space=pltpu.SMEM)],
    )
    entry, fresh, bent = [None] * CHUNKS, [None] * CHUNKS, [None] * CHUNKS
    arrived = [passed_along(leaving, one_on)]
    plain = [wide(jnp.bfloat16), wide(jnp.float32), wide(jnp.bfloat16)]
    for chunk in range(1, CHUNKS):
        leaving = call(functools.partial(pass_kernel, False), narrow, plain, starts[chunk], starts[chunk], w, p)
        arrived.append(passed_along(leaving, one_on))
    for chunk in range(CHUNKS):
        leaving = call(functools.partial(pass_kernel, False), narrow, plain, starts[chunk], arrived[chunk], w, p)
        entry[chunk] = passed_along(leaving, one_on)
    for chunk in range(CHUNKS):
        leaving, bent[chunk] = call(
            functools.partial(pass_kernel, True),
            (narrow, kept((rows, width), jnp.float32)), plain, starts[chunk], entry[chunk], w, p,
        )
        fresh[chunk] = passed_along(leaving, one_on)
    moved = [None] * CHUNKS
    group_index = lax.axis_index("depth") // INTERVAL
    for group in range(1, groups - 1):
        ahead = [(source, source + INTERVAL) for source in range(group * INTERVAL, (group + 1) * INTERVAL)]
        for chunk in range(CHUNKS):
            operands = [starts[chunk], entry[chunk], fresh[chunk]]
            if group > 1:
                operands.append(moved[chunk])
            delta = call(
                functools.partial(coarse_kernel, group), narrow,
                [wide(jnp.bfloat16)] * 3, *operands, bent[chunk], w, p, layers=1,
            )
            sent = passed_along(delta, ahead)
            moved[chunk] = sent if group == 1 else jnp.where(group_index == group + 1, sent, moved[chunk])
    outs = []
    for chunk in range(CHUNKS):
        outs.append(
            call(
                final_kernel, jax.ShapeDtypeStruct((2, rows, width), jnp.bfloat16),
                [wide(jnp.bfloat16), wide(jnp.bfloat16), wide(jnp.float32), wide(jnp.bfloat16)],
                starts[chunk], entry[chunk], fresh[chunk], moved[chunk], w, p,
            )
        )
    states = jnp.concatenate(outs, axis=1)
    return states.reshape(states.shape[0], initial.shape[0], -1, width)


def solution(mesh):
    placed = (P(), P("depth", None, None), P("depth", None), P("depth"))
    return jax.shard_map(
        local, mesh=mesh, in_specs=placed, out_specs=P("depth", None, None, None), check_vma=False
    )
```

```python
import functools

import jax
import jax.numpy as jnp
from jax import lax
from jax.experimental import pallas as pl
from jax.experimental.pallas import tpu as pltpu
from jax.sharding import PartitionSpec as P

LAY_DEV = 2
INTERVAL = 8

SHARES = (4, 4, 4, 4)
PASSES = (0, 1, 0, 2, 1, 0, 3, 1, 2, 3, 2, 3)
FIRST_LAG = 2.5
NEXT_LAG = 3.2
TILE = 512
VMEM_BYTES = 20 << 20
VMEM = pl.BlockSpec(memory_space=pltpu.VMEM)
ANY = pl.BlockSpec(memory_space=pl.ANY)
DMA = pltpu.SemaphoreType.DMA


def held(value):
    return pltpu.with_memory_space_constraint(value, pltpu.VMEM)


def kept(shape, kind):
    return pltpu.VMEM(shape, kind)


def in_hbm(value):
    return pltpu.with_memory_space_constraint(value, pltpu.HBM)


def passed_along(value, pairs):
    return lax.ppermute(value, "depth", pairs)


def tiles(width):
    tile = TILE if width % TILE == 0 else width
    return [slice(low, low + tile) for low in range(0, width, tile)]


def bend(state, w_ref, p_ref, layer, cols):
    pre = jnp.dot(state, w_ref[layer, :, cols], preferred_element_type=jnp.float32)
    return jnp.tanh(pre + p_ref[layer : layer + 1, cols])


def opening_kernel(rows, start_hbm, w_hbm, b_hbm, h_hbm, out_ref, start_ref, w_ref, p_ref, state, rounded, b_ref, h_ref, w_sems, sems):
    width = w_hbm.shape[2]
    small = [
        pltpu.make_async_copy(start_hbm, start_ref, sems.at[0]),
        pltpu.make_async_copy(b_hbm, b_ref, sems.at[1]),
        pltpu.make_async_copy(h_hbm, h_ref, sems.at[2]),
    ]
    for copy in small:
        copy.start()
    copies = []
    for layer in range(LAY_DEV):
        for cols in tiles(width):
            copy = pltpu.make_async_copy(
                w_hbm.at[layer, :, cols], w_ref.at[layer, :, cols], w_sems.at[len(copies)]
            )
            copy.start()
            copies.append(copy)
    for copy in small:
        copy.wait()
    p_ref[0:2, :] = b_ref[...]
    for layer in range(LAY_DEV):
        p_ref[2 + layer : 3 + layer, :] = jnp.full((1, width), h_ref[layer], jnp.float32)
    p_ref[4:8, :] = jnp.zeros((4, width), jnp.float32)
    start = start_ref[rows, :]
    for index, cols in enumerate(tiles(width)):
        copies[index].wait()
        moved = start[:, cols].astype(jnp.float32) + p_ref[2:3, cols] * bend(start, w_ref, p_ref, 0, cols)
        state[:, cols] = moved
        rounded[:, cols] = moved.astype(jnp.bfloat16)
    for index, cols in enumerate(tiles(width)):
        copies[len(tiles(width)) + index].wait()
        bent = bend(rounded[...], w_ref, p_ref, 1, cols)
        out_ref[:, cols] = (state[:, cols] + p_ref[3:4, cols] * bent).astype(jnp.bfloat16)


def pass_kernel(rows, opening, keep, after_ref, start_ref, w_ref, p_ref, *rest):
    if opening:
        out_ref, state, rounded = rest
        entering = start_ref.at[rows, :]
    else:
        arrived_ref, *rest = rest
        if keep:
            out_ref, t_ref, entering, state, rounded = rest
        else:
            out_ref, entering, state, rounded = rest
        entering[...] = jnp.where(lax.axis_index("depth") == 0, start_ref[rows, :], arrived_ref[...])
    for cols in tiles(w_ref.shape[2]):
        bent = bend(entering[...], w_ref, p_ref, 0, cols)
        if keep:
            t_ref[:, cols] = bent
        moved = entering[:, cols].astype(jnp.float32) + p_ref[2:3, cols] * bent
        state[:, cols] = moved
        rounded[:, cols] = moved.astype(jnp.bfloat16)
    for cols in tiles(w_ref.shape[2]):
        bent = bend(rounded[...], w_ref, p_ref, 1, cols)
        out_ref[:, cols] = (state[:, cols] + p_ref[3:4, cols] * bent).astype(jnp.bfloat16)


def correction_of(entry_ref, fresh_ref, moved_ref):
    total = fresh_ref[...].astype(jnp.float32) - entry_ref[...].astype(jnp.float32)
    if moved_ref is not None:
        total = moved_ref[...].astype(jnp.float32) + total
    return total.astype(jnp.bfloat16)


def coarse_kernel(group, after_ref, entry_ref, fresh_ref, t_ref, w_ref, p_ref, *rest):
    moved_ref = None
    if group > 1:
        moved_ref, before_ref, *rest = rest
    out_ref, correction_ref, rounded = rest

    here = lax.axis_index("depth") // INTERVAL == group
    if group > 1:

        @pl.when(jnp.logical_not(here))
        def _():
            correction_ref[...] = before_ref[...]

    @pl.when(here)
    def _():
        correction = correction_of(entry_ref, fresh_ref, moved_ref)
        correction_ref[...] = correction
        rounded[...] = (entry_ref[...].astype(jnp.float32) + correction.astype(jnp.float32)).astype(jnp.bfloat16)
        for cols in tiles(w_ref.shape[2]):
            bent = bend(rounded[...], w_ref, p_ref, 0, cols)
            change = (INTERVAL * LAY_DEV) * p_ref[2:3, cols] * (bent - t_ref[:, cols])
            out_ref[:, cols] = (correction_ref[:, cols].astype(jnp.float32) + change).astype(jnp.bfloat16)


def final_kernel(rows, groups, aliased, after_ref, start_ref, w_ref, p_ref, entry_ref, fresh_ref, moved_ref, correction_ref, *rest):
    if aliased:
        _, *rest = rest
    states, state, first, second, sems = rest
    device = lax.axis_index("depth")
    group = device // INTERVAL
    width = w_ref.shape[2]

    @pl.when(group == 0)
    def _():
        entry = jnp.where(device == 0, start_ref[rows, :], entry_ref[...])
        state[...] = entry.astype(jnp.float32)

    @pl.when((group > 0) & (group < groups - 1))
    def _():
        state[...] = entry_ref[...].astype(jnp.float32) + correction_ref[...].astype(jnp.float32)

    @pl.when((group > 0) & (group == groups - 1))
    def _():
        correction = correction_of(entry_ref, fresh_ref, moved_ref)
        state[...] = entry_ref[...].astype(jnp.float32) + correction.astype(jnp.float32)

    second[...] = state[...].astype(jnp.bfloat16)
    copies = []
    for cols in tiles(width):
        moved = state[:, cols] + p_ref[2:3, cols] * bend(second[...], w_ref, p_ref, 0, cols)
        state[:, cols] = moved
        first[:, cols] = moved.astype(jnp.bfloat16)
        copy = pltpu.make_async_copy(first.at[:, cols], states.at[0, rows, cols], sems.at[len(copies)])
        copy.start()
        copies.append(copy)
    for cols in tiles(width):
        bent = bend(first[...], w_ref, p_ref, 1, cols)
        second[:, cols] = (state[:, cols] + p_ref[3:4, cols] * bent).astype(jnp.bfloat16)
        copy = pltpu.make_async_copy(second.at[:, cols], states.at[1, rows, cols], sems.at[len(copies)])
        copy.start()
        copies.append(copy)
    for copy in copies:
        copy.wait()


def order_of(groups):
    chunks = len(SHARES)
    times, done = [], [0] * chunks
    for place, chunk in enumerate(PASSES):
        done[chunk] += 1
        times.append((place, 0, "pass", chunk, done[chunk] - 1))
        if done[chunk] == 3:
            due = place + FIRST_LAG
            for group in range(1, groups - 1):
                times.append((due, 1, "coarse", chunk, group))
                due += NEXT_LAG
            times.append((due, 2, "final", chunk, 0))
    return [item[2:] for item in sorted(times)]


def local(initial, weights, biases, step_sizes):
    count = lax.axis_size("depth")
    groups = count // INTERVAL
    width = initial.shape[2]
    start_hbm = initial.reshape(-1, width)
    total = start_hbm.shape[0]
    bounds = [0]
    for share in SHARES:
        bounds.append(bounds[-1] + share * total // sum(SHARES))
    spans = [slice(low, high) for low, high in zip(bounds, bounds[1:])]
    sizes = [span.stop - span.start for span in spans]
    parts = len(tiles(width))
    one_on = [(source, source + 1) for source in range(count - 1)]

    def narrow(size):
        return kept((size, width), jnp.bfloat16)

    def call(body, size, layers, outs, out_specs, scratch, operands, specs, aliases=None):
        return pl.pallas_call(
            body,
            out_shape=outs,
            in_specs=specs,
            out_specs=out_specs,
            scratch_shapes=scratch,
            input_output_aliases=aliases or {},
            compiler_params=pltpu.CompilerParams(vmem_limit_bytes=VMEM_BYTES),
            cost_estimate=pl.CostEstimate(
                flops=2 * size * width * width * layers,
                bytes_accessed=size * width * 8,
                transcendentals=size * width * layers,
            ),
        )(*[held(value) if spec is VMEM else in_hbm(value) for value, spec in zip(operands, specs)])

    first = sizes[0]
    leaving, start, w, p = call(
        functools.partial(opening_kernel, spans[0]), first, LAY_DEV,
        (narrow(first), narrow(total), kept(weights.shape, jnp.bfloat16), kept((8, width), jnp.float32)),
        (VMEM,) * 4,
        [
            pltpu.VMEM((first, width), jnp.float32), pltpu.VMEM((first, width), jnp.bfloat16),
            pltpu.VMEM(biases.shape, jnp.float32), pltpu.SMEM(step_sizes.shape, jnp.float32),
            DMA((LAY_DEV * parts,)), DMA((3,)),
        ],
        [start_hbm, weights, biases, step_sizes], [ANY] * 4,
    )
    chunks = len(SHARES)
    bent, correction, moved = [None] * chunks, [None] * chunks, [None] * chunks
    arrived = [[] for _ in range(chunks)]
    arrived[0].append(passed_along(leaving, one_on))
    after, after_spec, states = leaving, VMEM, None
    for kind, chunk, step in order_of(groups)[1:]:
        size = sizes[chunk]
        wide = pltpu.VMEM((size, width), jnp.float32)
        thin = pltpu.VMEM((size, width), jnp.bfloat16)
        if kind == "pass":
            keep = step == 2
            operands = [after, start, w, p] + ([arrived[chunk][-1]] if step else [])
            result = call(
                functools.partial(pass_kernel, spans[chunk], step == 0, keep), size, LAY_DEV,
                (narrow(size), kept((size, width), jnp.float32)) if keep else narrow(size),
                (VMEM, VMEM) if keep else VMEM,
                [thin, wide, thin] if step else [wide, thin],
                operands, [after_spec] + [VMEM] * (len(operands) - 1),
            )
            if keep:
                leaving, bent[chunk] = result
            else:
                leaving = result
            arrived[chunk].append(passed_along(leaving, one_on))
            after, after_spec = leaving, VMEM
        elif kind == "coarse":
            _, entry, fresh = arrived[chunk]
            operands = [after, entry, fresh, bent[chunk], w, p]
            if step > 1:
                operands += [moved[chunk], correction[chunk]]
            delta, correction[chunk] = call(
                functools.partial(coarse_kernel, step), size, 1,
                (narrow(size), narrow(size)), (VMEM, VMEM), [thin],
                operands, [after_spec] + [VMEM] * (len(operands) - 1),
            )
            ahead = [(source, source + INTERVAL) for source in range(step * INTERVAL, (step + 1) * INTERVAL)]
            moved[chunk] = passed_along(delta, ahead)
            after, after_spec = delta, VMEM
        else:
            _, entry, fresh = arrived[chunk]
            operands = [after, start, w, p, entry, fresh, moved[chunk], correction[chunk]]
            specs = [after_spec] + [VMEM] * (len(operands) - 1)
            aliases = None
            if states is not None:
                aliases = {len(operands): 0}
                operands.append(states)
                specs.append(ANY)
                if after_spec is ANY:
                    operands[0], specs[0] = start, VMEM
            states = call(
                functools.partial(final_kernel, spans[chunk], groups, states is not None), size, LAY_DEV,
                jax.ShapeDtypeStruct((LAY_DEV, total, width), jnp.bfloat16), ANY,
                [wide, thin, thin, DMA((LAY_DEV * parts,))], operands, specs, aliases,
            )
            after, after_spec = states, ANY
    return states.reshape(LAY_DEV, initial.shape[0], -1, width)


def solution(mesh):
    placed = (P(), P("depth", None, None), P("depth", None), P("depth"))
    return jax.shard_map(
        local, mesh=mesh, in_specs=placed, out_specs=P("depth", None, None, None), check_vma=False
    )
```

```python
import functools

import jax
import jax.numpy as jnp
from jax import lax
from jax.experimental import pallas as pl
from jax.experimental.pallas import tpu as pltpu
from jax.sharding import PartitionSpec as P

LAY_DEV = 2
INTERVAL = 8

SHARES = (4, 5, 4, 3)
ORDER = (
    0, 20, 10, 1, 21, 11, 2, 30, 12, 3, 31, 22, 13, 17, 4, 32, 23, 14, 33, 5, 24, 34, 15, 25, 35,
)
RELAYS = {8: (0, 2), 6: (1, 6), 7: (2, 2)}
TILE = 512
VMEM_BYTES = 20 << 20
VMEM = pl.BlockSpec(memory_space=pltpu.VMEM)
ANY = pl.BlockSpec(memory_space=pl.ANY)
DMA = pltpu.SemaphoreType.DMA


def held(value):
    return pltpu.with_memory_space_constraint(value, pltpu.VMEM)


def kept(shape, kind):
    return pltpu.VMEM(shape, kind)


def in_hbm(value):
    return pltpu.with_memory_space_constraint(value, pltpu.HBM)


def passed_along(value, pairs):
    return lax.ppermute(value, "depth", pairs)


def tiles(width):
    tile = TILE if width % TILE == 0 else width
    return [slice(low, low + tile) for low in range(0, width, tile)]


def bend(state, w_ref, p_ref, layer, cols):
    pre = jnp.dot(state, w_ref[layer, :, cols], preferred_element_type=jnp.float32)
    return jnp.tanh(pre + p_ref[layer : layer + 1, cols])


def opening_kernel(rows, start_hbm, w_hbm, b_hbm, h_hbm, out_ref, w_ref, p_ref, start, state, rounded, b_ref, h_ref, w_sems, sems):
    width = w_hbm.shape[2]
    small = [
        pltpu.make_async_copy(start_hbm.at[rows, :], start, sems.at[0]),
        pltpu.make_async_copy(b_hbm, b_ref, sems.at[1]),
        pltpu.make_async_copy(h_hbm, h_ref, sems.at[2]),
    ]
    for copy in small:
        copy.start()
    copies = []
    for layer in range(LAY_DEV):
        for cols in tiles(width):
            copy = pltpu.make_async_copy(
                w_hbm.at[layer, :, cols], w_ref.at[layer, :, cols], w_sems.at[len(copies)]
            )
            copy.start()
            copies.append(copy)
    for copy in small:
        copy.wait()
    p_ref[0:2, :] = b_ref[...]
    for layer in range(LAY_DEV):
        p_ref[2 + layer : 3 + layer, :] = jnp.full((1, width), h_ref[layer], jnp.float32)
    p_ref[4:8, :] = jnp.zeros((4, width), jnp.float32)
    for index, cols in enumerate(tiles(width)):
        copies[index].wait()
        moved = start[:, cols].astype(jnp.float32) + p_ref[2:3, cols] * bend(start[...], w_ref, p_ref, 0, cols)
        state[:, cols] = moved
        rounded[:, cols] = moved.astype(jnp.bfloat16)
    for index, cols in enumerate(tiles(width)):
        copies[len(tiles(width)) + index].wait()
        bent = bend(rounded[...], w_ref, p_ref, 1, cols)
        out_ref[:, cols] = (state[:, cols] + p_ref[3:4, cols] * bent).astype(jnp.bfloat16)


def total_of(parts):
    return sum(part[...].astype(jnp.float32) for part in parts)


def pass_kernel(rows, parts, keep, extra, start_ref, w_ref, p_ref, *rest):
    arrived, rest = rest[:parts], rest[parts + extra :]
    if parts:
        if keep:
            out_ref, t_ref, entering, state, rounded = rest
        else:
            out_ref, entering, state, rounded = rest
        came = total_of(arrived).astype(jnp.bfloat16) if parts > 1 else arrived[0][...]
        entering[...] = jnp.where(lax.axis_index("depth") == 0, start_ref[rows, :], came)
    else:
        out_ref, state, rounded = rest
        entering = start_ref.at[rows, :]
    for cols in tiles(w_ref.shape[2]):
        bent = bend(entering[...], w_ref, p_ref, 0, cols)
        if keep:
            t_ref[:, cols] = bent
        moved = entering[:, cols].astype(jnp.float32) + p_ref[2:3, cols] * bent
        state[:, cols] = moved
        rounded[:, cols] = moved.astype(jnp.bfloat16)
    for cols in tiles(w_ref.shape[2]):
        bent = bend(rounded[...], w_ref, p_ref, 1, cols)
        out_ref[:, cols] = (state[:, cols] + p_ref[3:4, cols] * bent).astype(jnp.bfloat16)


def relay_kernel(place, extra, came_ref, *rest):
    (out_ref,) = rest[extra:]

    @pl.when(lax.axis_index("depth") % INTERVAL == place)
    def _():
        out_ref[...] = came_ref[...]


def correction_of(entry, fresh, moved_ref):
    total = fresh - entry
    if moved_ref is not None:
        total = moved_ref[...].astype(jnp.float32) + total
    return total.astype(jnp.bfloat16)


def coarse_kernel(group, extra, parts, t_ref, w_ref, p_ref, *rest):
    (entry_parts, fresh_parts), rest = parts, rest
    entry_refs, rest = rest[:entry_parts], rest[entry_parts:]
    fresh_refs, rest = rest[:fresh_parts], rest[fresh_parts:]
    moved_ref = None
    if group > 1:
        moved_ref, before_ref, *rest = rest
    out_ref, correction_ref, rounded = rest[extra:]

    here = lax.axis_index("depth") // INTERVAL == group
    if group > 1:

        @pl.when(jnp.logical_not(here))
        def _():
            correction_ref[...] = before_ref[...]

    @pl.when(here)
    def _():
        entry = total_of(entry_refs)
        correction = correction_of(entry, total_of(fresh_refs), moved_ref)
        correction_ref[...] = correction
        rounded[...] = (entry + correction.astype(jnp.float32)).astype(jnp.bfloat16)
        for cols in tiles(w_ref.shape[2]):
            bent = bend(rounded[...], w_ref, p_ref, 0, cols)
            change = (INTERVAL * LAY_DEV) * p_ref[2:3, cols] * (bent - t_ref[:, cols])
            out_ref[:, cols] = (correction_ref[:, cols].astype(jnp.float32) + change).astype(jnp.bfloat16)


def final_kernel(rows, groups, aliased, extra, parts, start_ref, w_ref, p_ref, moved_ref, correction_ref, *rest):
    entry_parts, fresh_parts = parts
    entry_refs, rest = rest[:entry_parts], rest[entry_parts:]
    fresh_refs, rest = rest[:fresh_parts], rest[fresh_parts + int(aliased) + extra :]
    states, token, state, first, second, sems = rest
    token[...] = jnp.zeros_like(token)
    device = lax.axis_index("depth")
    group = device // INTERVAL
    width = w_ref.shape[2]

    entry = total_of(entry_refs)

    @pl.when(group == 0)
    def _():
        state[...] = jnp.where(device == 0, start_ref[rows, :].astype(jnp.float32), entry)

    @pl.when((group > 0) & (group < groups - 1))
    def _():
        state[...] = entry + correction_ref[...].astype(jnp.float32)

    @pl.when((group > 0) & (group == groups - 1))
    def _():
        state[...] = entry + correction_of(entry, total_of(fresh_refs), moved_ref).astype(jnp.float32)

    second[...] = state[...].astype(jnp.bfloat16)
    copies = []
    for cols in tiles(width):
        moved = state[:, cols] + p_ref[2:3, cols] * bend(second[...], w_ref, p_ref, 0, cols)
        state[:, cols] = moved
        first[:, cols] = moved.astype(jnp.bfloat16)
        copy = pltpu.make_async_copy(first.at[:, cols], states.at[0, rows, cols], sems.at[len(copies)])
        copy.start()
        copies.append(copy)
    for cols in tiles(width):
        bent = bend(first[...], w_ref, p_ref, 1, cols)
        second[:, cols] = (state[:, cols] + p_ref[3:4, cols] * bent).astype(jnp.bfloat16)
        copy = pltpu.make_async_copy(second.at[:, cols], states.at[1, rows, cols], sems.at[len(copies)])
        copy.start()
        copies.append(copy)
    for copy in copies:
        copy.wait()


def order_of(groups):
    order, late = [], []
    for item in ORDER:
        chunk, step = divmod(item, 10)
        if step < 3:
            order.append(("pass", chunk, step))
        elif step in RELAYS:
            order.append(("relay", chunk, step))
        elif step < 5:
            if step - 2 < groups - 1:
                order.append(("coarse", chunk, step - 2))
        elif groups > 4:
            late.append(("final", chunk, 0))
        else:
            order.append(("final", chunk, 0))
    for group in range(3, groups - 1):
        order += [("coarse", chunk, group) for _, chunk, _ in late]
    return order + late


def local(initial, weights, biases, step_sizes):
    count = lax.axis_size("depth")
    groups = count // INTERVAL
    width = initial.shape[2]
    start = initial.reshape(-1, width)
    total = start.shape[0]
    bounds = [0]
    for share in SHARES:
        bounds.append(bounds[-1] + share * total // sum(SHARES))
    spans = [slice(low, high) for low, high in zip(bounds, bounds[1:])]
    sizes = [span.stop - span.start for span in spans]
    parts = len(tiles(width))
    one_on = [(source, source + 1) for source in range(count - 1)]
    ends = range(2 * INTERVAL - 1, count - 1, INTERVAL)
    straight = [pair for pair in one_on if pair[0] not in ends]

    def narrow(size):
        return kept((size, width), jnp.bfloat16)

    def call(body, outs, scratch, operands, specs=None, out_specs=None, aliases=None):
        specs = specs or [VMEM] * len(operands)
        return pl.pallas_call(
            body,
            out_shape=outs,
            in_specs=specs,
            out_specs=out_specs or jax.tree.map(lambda _: VMEM, outs),
            scratch_shapes=scratch,
            input_output_aliases=aliases or {},
            compiler_params=pltpu.CompilerParams(vmem_limit_bytes=VMEM_BYTES),
            cost_estimate=pl.CostEstimate(
                flops=2 * LAY_DEV * total * width * width, bytes_accessed=0, transcendentals=0
            ),
        )(*[held(value) if spec is VMEM else in_hbm(value) for value, spec in zip(operands, specs)])

    first = sizes[0]
    leaving, w, p = call(
        functools.partial(opening_kernel, spans[0]),
        (narrow(first), kept(weights.shape, jnp.bfloat16), kept((8, width), jnp.float32)),
        [
            pltpu.VMEM((first, width), jnp.bfloat16),
            pltpu.VMEM((first, width), jnp.float32), pltpu.VMEM((first, width), jnp.bfloat16),
            pltpu.VMEM(biases.shape, jnp.float32), pltpu.SMEM(step_sizes.shape, jnp.float32),
            DMA((LAY_DEV * parts,)), DMA((3,)),
        ],
        [start, weights, biases, step_sizes], [ANY] * 4,
    )
    chunks = len(SHARES)
    bent, correction, moved = [None] * chunks, [None] * chunks, [None] * chunks
    arrived = [[] for _ in range(chunks)]
    asides, underway = {}, []
    relayed = {(item // 10, RELAYS[item % 10][0]): item % 10 for item in ORDER if item % 10 in RELAYS}

    def sent(value, pairs):
        underway.append(passed_along(value, pairs))
        return underway[-1]

    def passed(value, chunk, step):
        kind = relayed.get((chunk, step))
        if kind is None:
            arrived[chunk].append([sent(value, one_on)])
        else:
            back = RELAYS[kind][1]
            arrived[chunk].append([sent(value, straight)])
            asides[chunk, step] = sent(value, [(end, end - back) for end in ends])

    def earlier(values):
        found = []
        for value in values:
            if any(value is other for other in underway):
                while True:
                    oldest = underway.pop(0)
                    if oldest is value:
                        break
                    found.append(oldest)
        return [other for other in found if not any(other is value for value in values)]

    passed(leaving, 0, 0)
    after, states = [leaving], None
    for kind, chunk, step in order_of(groups)[1:]:
        size = sizes[chunk]
        wide = pltpu.VMEM((size, width), jnp.float32)
        thin = pltpu.VMEM((size, width), jnp.bfloat16)
        if kind == "pass":
            keep = step == 2
            came = arrived[chunk][step - 1] if step else []
            extra = after + earlier(came)
            result = call(
                functools.partial(pass_kernel, spans[chunk], len(came), keep, len(extra)),
                (narrow(size), kept((size, width), jnp.float32)) if keep else narrow(size),
                [thin, wide, thin] if step else [wide, thin],
                [start, w, p] + came + extra,
            )
            if keep:
                leaving, bent[chunk] = result
            else:
                leaving = result
            passed(leaving, chunk, step)
            after = [leaving]
        elif kind == "relay":
            step, back = RELAYS[step]
            came = asides[chunk, step]
            extra = after + earlier([came])
            leaving = call(
                functools.partial(relay_kernel, INTERVAL - 1 - back, len(extra)), narrow(size), [], [came] + extra
            )
            arrived[chunk][step].append(sent(leaving, [(end - back, end + 1) for end in ends]))
            after = [leaving]
        elif kind == "coarse":
            _, entry, fresh = arrived[chunk]
            if step == 1:
                fresh = fresh[:1]
            operands = [bent[chunk], w, p] + entry + fresh
            needed = entry + fresh
            if step > 1:
                operands += [moved[chunk], correction[chunk]]
                needed = needed + [moved[chunk]]
            extra = after + earlier(needed)
            delta, correction[chunk] = call(
                functools.partial(coarse_kernel, step, len(extra), (len(entry), len(fresh))),
                (narrow(size), narrow(size)), [thin], operands + extra,
            )
            ahead = [(source, source + INTERVAL) for source in range(step * INTERVAL, (step + 1) * INTERVAL)]
            moved[chunk] = sent(delta, ahead)
            after = [delta]
        else:
            _, entry, fresh = arrived[chunk]
            extra = after + earlier([moved[chunk]])
            operands = [start, w, p, moved[chunk], correction[chunk]] + entry + fresh
            specs = [VMEM] * len(operands)
            aliases = None
            if states is not None:
                aliases = {len(operands): 0}
                operands.append(states)
                specs.append(ANY)
            states, token = call(
                functools.partial(
                    final_kernel, spans[chunk], groups, states is not None, len(extra), (len(entry), len(fresh))
                ),
                (jax.ShapeDtypeStruct((LAY_DEV, total, width), jnp.bfloat16), kept((8, 128), jnp.float32)),
                [wide, thin, thin, DMA((LAY_DEV * parts,))],
                operands + extra, specs + [VMEM] * len(extra), (ANY, VMEM), aliases,
            )
            after = [token]
    return states.reshape(LAY_DEV, initial.shape[0], -1, width)


def solution(mesh):
    placed = (P(), P("depth", None, None), P("depth", None), P("depth"))
    return jax.shard_map(
        local, mesh=mesh, in_specs=placed, out_specs=P("depth", None, None, None), check_vma=False
    )
```

```python
import functools

import jax
import jax.numpy as jnp
from jax import lax
from jax.experimental import pallas as pl
from jax.experimental.pallas import tpu as pltpu
from jax.sharding import PartitionSpec as P

LAY_DEV = 2
INTERVAL = 8

SHARES = (5, 4, 4, 3)
ORDER = (
    0, 20, 10, 1, 21, 11, 2, 30, 12, 3, 31, 22, 13, 4, 23, 28, 32, 14, 5, 24, 33, 15, 34, 25, 35,
)
RELAYS = {7: 2, 8: 4}
APART = ()
UNDERWAY = 5
TILE = 512
ROWS_AT_ONCE = 128
VMEM_BYTES = 20 << 20
VMEM = pl.BlockSpec(memory_space=pltpu.VMEM)
ANY = pl.BlockSpec(memory_space=pl.ANY)
DMA = pltpu.SemaphoreType.DMA


def held(value):
    return pltpu.with_memory_space_constraint(value, pltpu.VMEM)


def kept(shape, kind):
    return pltpu.VMEM(shape, kind)


def in_hbm(value):
    return pltpu.with_memory_space_constraint(value, pltpu.HBM)


def passed_along(value, pairs):
    return lax.ppermute(value, "depth", pairs)


def tiles(width):
    tile = TILE if width % TILE == 0 else width
    return [slice(low, low + tile) for low in range(0, width, tile)]


def bend(state, size, w_ref, p_ref, layer, cols):
    pre = jnp.dot(state, w_ref[layer, :, cols], preferred_element_type=jnp.float32)
    return jnp.tanh(pre[:size] + p_ref[layer : layer + 1, cols])


def opening_kernel(rows, start_hbm, w_hbm, b_hbm, h_hbm, out_ref, w_ref, p_ref, start, state, rounded, b_ref, h_ref, w_sems, sems):
    width, size = w_hbm.shape[2], out_ref.shape[0]
    small = [
        pltpu.make_async_copy(start_hbm.at[rows, :], start, sems.at[0]),
        pltpu.make_async_copy(b_hbm, b_ref, sems.at[1]),
        pltpu.make_async_copy(h_hbm, h_ref, sems.at[2]),
    ]
    for copy in small:
        copy.start()
    copies = []
    for layer in range(LAY_DEV):
        for cols in tiles(width):
            copy = pltpu.make_async_copy(
                w_hbm.at[layer, :, cols], w_ref.at[layer, :, cols], w_sems.at[len(copies)]
            )
            copy.start()
            copies.append(copy)
    for copy in small:
        copy.wait()
    p_ref[0:2, :] = b_ref[...]
    for layer in range(LAY_DEV):
        p_ref[2 + layer : 3 + layer, :] = jnp.full((1, width), h_ref[layer], jnp.float32)
    p_ref[4:8, :] = jnp.zeros((4, width), jnp.float32)
    for index, cols in enumerate(tiles(width)):
        copies[index].wait()
        moved = start[:, cols].astype(jnp.float32) + p_ref[2:3, cols] * bend(start[...], size, w_ref, p_ref, 0, cols)
        state[:, cols] = moved
        rounded[:, cols] = moved.astype(jnp.bfloat16)
    for index, cols in enumerate(tiles(width)):
        copies[len(tiles(width)) + index].wait()
        bent = bend(rounded[...], size, w_ref, p_ref, 1, cols)
        out_ref[:, cols] = (state[:, cols] + p_ref[3:4, cols] * bent).astype(jnp.bfloat16)


def total_of(parts):
    return sum(part[...].astype(jnp.float32) for part in parts)


def pass_kernel(rows, parts, keep, extra, start_ref, w_ref, p_ref, *rest):
    arrived, rest = rest[:parts], rest[parts + extra :]
    t_ref = None
    if keep:
        out_ref, t_ref, entering, state, rounded = rest
    else:
        out_ref, entering, state, rounded = rest
    size = out_ref.shape[0]
    if parts:
        came = total_of(arrived).astype(jnp.bfloat16) if parts > 1 else arrived[0][...]
        entering[:size] = jnp.where(lax.axis_index("depth") == 0, start_ref[rows, :], came)
    else:
        entering[:size] = start_ref[rows, :]
    for cols in tiles(w_ref.shape[2]):
        bent = bend(entering[...], size, w_ref, p_ref, 0, cols)
        if keep:
            t_ref[:, cols] = bent
        moved = entering[:size, cols].astype(jnp.float32) + p_ref[2:3, cols] * bent
        state[:, cols] = moved
        rounded[:size, cols] = moved.astype(jnp.bfloat16)
    for cols in tiles(w_ref.shape[2]):
        bent = bend(rounded[...], size, w_ref, p_ref, 1, cols)
        out_ref[:, cols] = (state[:, cols] + p_ref[3:4, cols] * bent).astype(jnp.bfloat16)


def relay_kernel(place, extra, came_ref, *rest):
    (out_ref,) = rest[extra:]

    @pl.when(lax.axis_index("depth") % INTERVAL == place)
    def _():
        out_ref[...] = came_ref[...]


def correction_of(entry, fresh, moved_ref):
    total = fresh - entry
    if moved_ref is not None:
        total = moved_ref[...].astype(jnp.float32) + total
    return total.astype(jnp.bfloat16)


def coarse_kernel(group, extra, parts, t_ref, w_ref, p_ref, *rest):
    (entry_parts, fresh_parts), rest = parts, rest
    entry_refs, rest = rest[:entry_parts], rest[entry_parts:]
    fresh_refs, rest = rest[:fresh_parts], rest[fresh_parts:]
    moved_ref = None
    if group > 1:
        moved_ref, before_ref, *rest = rest
    out_ref, correction_ref, rounded = rest[extra:]

    here = lax.axis_index("depth") // INTERVAL == group
    if group > 1:

        @pl.when(jnp.logical_not(here))
        def _():
            correction_ref[...] = before_ref[...]

    @pl.when(here)
    def _():
        entry = total_of(entry_refs)
        correction = correction_of(entry, total_of(fresh_refs), moved_ref)
        correction_ref[...] = correction
        size = out_ref.shape[0]
        rounded[:size] = (entry + correction.astype(jnp.float32)).astype(jnp.bfloat16)
        for cols in tiles(w_ref.shape[2]):
            bent = bend(rounded[...], size, w_ref, p_ref, 0, cols)
            change = (INTERVAL * LAY_DEV) * p_ref[2:3, cols] * (bent - t_ref[:, cols])
            out_ref[:, cols] = (correction_ref[:, cols].astype(jnp.float32) + change).astype(jnp.bfloat16)


def final_kernel(rows, groups, aliased, extra, parts, start_ref, w_ref, p_ref, moved_ref, correction_ref, *rest):
    entry_parts, fresh_parts = parts
    entry_refs, rest = rest[:entry_parts], rest[entry_parts:]
    fresh_refs, rest = rest[:fresh_parts], rest[fresh_parts + int(aliased) + extra :]
    states, token, state, first, second, sems = rest
    token[...] = jnp.zeros_like(token)
    device = lax.axis_index("depth")
    group = device // INTERVAL
    width = w_ref.shape[2]

    entry = total_of(entry_refs)

    @pl.when(group == 0)
    def _():
        state[...] = jnp.where(device == 0, start_ref[rows, :].astype(jnp.float32), entry)

    @pl.when((group > 0) & (group < groups - 1))
    def _():
        state[...] = entry + correction_ref[...].astype(jnp.float32)

    @pl.when((group > 0) & (group == groups - 1))
    def _():
        state[...] = entry + correction_of(entry, total_of(fresh_refs), moved_ref).astype(jnp.float32)

    size = state.shape[0]
    second[:size] = state[...].astype(jnp.bfloat16)
    copies = []

    def written(ref, layer, cols):
        copy = pltpu.make_async_copy(ref.at[:size, cols], states.at[layer, rows, cols], sems.at[len(copies)])
        copy.start()
        copies.append(copy)

    for cols in tiles(width):
        moved = state[:, cols] + p_ref[2:3, cols] * bend(second[...], size, w_ref, p_ref, 0, cols)
        state[:, cols] = moved
        first[:size, cols] = moved.astype(jnp.bfloat16)
        written(first, 0, cols)
    for cols in tiles(width):
        bent = bend(first[...], size, w_ref, p_ref, 1, cols)
        second[:size, cols] = (state[:, cols] + p_ref[3:4, cols] * bent).astype(jnp.bfloat16)
        written(second, 1, cols)
    for copy in copies:
        copy.wait()


def room_of(size):
    return ROWS_AT_ONCE if ROWS_AT_ONCE // 2 < size < ROWS_AT_ONCE else size


def order_of(groups):
    order, late = [], []
    for item in ORDER:
        chunk, step = divmod(item, 10)
        if step < 3:
            order.append(("pass", chunk, step))
        elif step in RELAYS:
            order.append(("relay", chunk, step))
        elif step < 5:
            if step - 2 < groups - 1:
                order.append(("coarse", chunk, step - 2))
        elif groups > 4:
            late.append(("final", chunk, 0))
        else:
            order.append(("final", chunk, 0))
    for group in range(3, groups - 1):
        order += [("coarse", chunk, group) for _, chunk, _ in late]
    return order + late


def local(initial, weights, biases, step_sizes):
    count = lax.axis_size("depth")
    groups = count // INTERVAL
    width = initial.shape[2]
    start = initial.reshape(-1, width)
    total = start.shape[0]
    bounds = [0]
    for share in SHARES:
        bounds.append(bounds[-1] + share * total // sum(SHARES))
    spans = [slice(low, high) for low, high in zip(bounds, bounds[1:])]
    sizes = [span.stop - span.start for span in spans]
    parts = len(tiles(width))
    one_on = [(source, source + 1) for source in range(count - 1)]
    ends = range(2 * INTERVAL - 1, count - 1, INTERVAL)
    straight = [pair for pair in one_on if pair[0] not in ends]

    def narrow(size):
        return kept((size, width), jnp.bfloat16)

    def call(body, outs, scratch, operands, specs=None, out_specs=None, aliases=None):
        specs = specs or [VMEM] * len(operands)
        return pl.pallas_call(
            body,
            out_shape=outs,
            in_specs=specs,
            out_specs=out_specs or jax.tree.map(lambda _: VMEM, outs),
            scratch_shapes=scratch,
            input_output_aliases=aliases or {},
            compiler_params=pltpu.CompilerParams(vmem_limit_bytes=VMEM_BYTES),
            cost_estimate=pl.CostEstimate(
                flops=2 * LAY_DEV * total * width * width, bytes_accessed=0, transcendentals=0
            ),
        )(*[held(value) if spec is VMEM else in_hbm(value) for value, spec in zip(operands, specs)])

    first = sizes[0]
    leaving, w, p = call(
        functools.partial(opening_kernel, spans[0]),
        (narrow(first), kept(weights.shape, jnp.bfloat16), kept((8, width), jnp.float32)),
        [
            pltpu.VMEM((first, width), jnp.bfloat16),
            pltpu.VMEM((first, width), jnp.float32), pltpu.VMEM((first, width), jnp.bfloat16),
            pltpu.VMEM(biases.shape, jnp.float32), pltpu.SMEM(step_sizes.shape, jnp.float32),
            DMA((LAY_DEV * parts,)), DMA((3,)),
        ],
        [start, weights, biases, step_sizes], [ANY] * 4,
    )
    chunks = len(SHARES)
    bent, correction, moved = [None] * chunks, [None] * chunks, [None] * chunks
    arrived = [[] for _ in range(chunks)]
    asides = {}
    back = {item // 10: RELAYS[item % 10] for item in ORDER if item % 10 in RELAYS}
    underway = []

    def sent(value, pairs):
        underway.append(passed_along(value, pairs))
        return underway[-1]

    def waited(values, sends):
        underway[:] = [other for other in underway if not any(other is value for value in values)]
        surplus = max(0, len(underway) + sends - UNDERWAY)
        oldest, underway[:] = underway[:surplus], underway[surplus:]
        return oldest

    def passed(value, chunk, step):
        if step == 2 and chunk in back:
            arrived[chunk].append([sent(value, straight)])
            asides[chunk] = sent(value, [(end, end - back[chunk]) for end in ends])
        elif step == 2 and chunk in APART:
            arrived[chunk].append([sent(value, straight), sent(value, [(end, end + 1) for end in ends])])
        else:
            arrived[chunk].append([sent(value, one_on)])

    passed(leaving, 0, 0)
    after, states = [leaving], None
    for kind, chunk, step in order_of(groups)[1:]:
        size = sizes[chunk]
        wide = pltpu.VMEM((size, width), jnp.float32)
        thin = pltpu.VMEM((room_of(size), width), jnp.bfloat16)
        if kind == "pass":
            keep = step == 2
            came = arrived[chunk][step - 1] if step else []
            after += waited(came, 2 if keep and (chunk in back or chunk in APART) else 1)
            result = call(
                functools.partial(pass_kernel, spans[chunk], len(came), keep, len(after)),
                (narrow(size), kept((size, width), jnp.float32)) if keep else narrow(size),
                [thin, wide, thin],
                [start, w, p] + came + after,
            )
            if keep:
                leaving, bent[chunk] = result
            else:
                leaving = result
            passed(leaving, chunk, step)
            after = [leaving]
        elif kind == "relay":
            came = [asides[chunk]]
            after += waited(came, 1)
            leaving = call(
                functools.partial(relay_kernel, INTERVAL - 1 - back[chunk], len(after)), narrow(size), [], came + after
            )
            arrived[chunk][2].append(sent(leaving, [(end - back[chunk], end + 1) for end in ends]))
            after = [leaving]
        elif kind == "coarse":
            _, entry, fresh = arrived[chunk]
            if step == 1:
                fresh = fresh[:1]
            operands = [bent[chunk], w, p] + entry + fresh
            if step > 1:
                operands += [moved[chunk], correction[chunk]]
            after += waited(operands, 1)
            delta, correction[chunk] = call(
                functools.partial(coarse_kernel, step, len(after), (len(entry), len(fresh))),
                (narrow(size), narrow(size)), [thin], operands + after,
            )
            ahead = [(source, source + INTERVAL) for source in range(step * INTERVAL, (step + 1) * INTERVAL)]
            moved[chunk] = sent(delta, ahead)
            after = [delta]
        else:
            _, entry, fresh = arrived[chunk]
            operands = [start, w, p, moved[chunk], correction[chunk]] + entry + fresh
            waited(operands, 0)
            specs = [VMEM] * len(operands)
            aliases = None
            if states is not None:
                aliases = {len(operands): 0}
                operands.append(states)
                specs.append(ANY)
            states, token = call(
                functools.partial(
                    final_kernel, spans[chunk], groups, states is not None, len(after), (len(entry), len(fresh))
                ),
                (jax.ShapeDtypeStruct((LAY_DEV, total, width), jnp.bfloat16), kept((8, 128), jnp.float32)),
                [wide, thin, thin, DMA((LAY_DEV * parts,))],
                operands + after, specs + [VMEM] * len(after), (ANY, VMEM), aliases,
            )
            after = [token]
    return states.reshape(LAY_DEV, initial.shape[0], -1, width)


def solution(mesh):
    placed = (P(), P("depth", None, None), P("depth", None), P("depth"))
    return jax.shard_map(
        local, mesh=mesh, in_specs=placed, out_specs=P("depth", None, None, None), check_vma=False
    )
```

```python
import functools

import jax
import jax.numpy as jnp
from jax import lax
from jax.experimental import pallas as pl
from jax.experimental.pallas import tpu as pltpu
from jax.sharding import PartitionSpec as P

LAY_DEV = 2
INTERVAL = 8

SHARES = (4, 5, 4, 3)
ORDER = (
    0, 20, 10, 1, 21, 11, 2, 30, 12, 3, 31, 22, 13, 17, 4, 32, 23, 14, 33, 5, 24, 34, 15, 25, 35,
)
RELAYS = {7: 2, 8: 4}
APART = ()
UNDERWAY = 5
TILE = 512
ROWS_AT_ONCE = 128
VMEM_BYTES = 20 << 20
VMEM = pl.BlockSpec(memory_space=pltpu.VMEM)
ANY = pl.BlockSpec(memory_space=pl.ANY)
DMA = pltpu.SemaphoreType.DMA


def held(value):
    return pltpu.with_memory_space_constraint(value, pltpu.VMEM)


def kept(shape, kind):
    return pltpu.VMEM(shape, kind)


def in_hbm(value):
    return pltpu.with_memory_space_constraint(value, pltpu.HBM)


def passed_along(value, pairs):
    return lax.ppermute(value, "depth", pairs)


def tiles(width):
    tile = TILE if width % TILE == 0 else width
    return [slice(low, low + tile) for low in range(0, width, tile)]


def bend(state, size, w_ref, p_ref, layer, cols):
    pre = jnp.dot(state, w_ref[layer, :, cols], preferred_element_type=jnp.float32)
    return jnp.tanh(pre[:size] + p_ref[layer : layer + 1, cols])


def opening_kernel(rows, start_hbm, w_hbm, b_hbm, h_hbm, out_ref, w_ref, p_ref, start, state, rounded, b_ref, h_ref, w_sems, sems):
    width, size = w_hbm.shape[2], out_ref.shape[0]
    small = [
        pltpu.make_async_copy(start_hbm.at[rows, :], start, sems.at[0]),
        pltpu.make_async_copy(b_hbm, b_ref, sems.at[1]),
        pltpu.make_async_copy(h_hbm, h_ref, sems.at[2]),
    ]
    for copy in small:
        copy.start()
    copies = []
    for layer in range(LAY_DEV):
        for cols in tiles(width):
            copy = pltpu.make_async_copy(
                w_hbm.at[layer, :, cols], w_ref.at[layer, :, cols], w_sems.at[len(copies)]
            )
            copy.start()
            copies.append(copy)
    for copy in small:
        copy.wait()
    p_ref[0:2, :] = b_ref[...]
    for layer in range(LAY_DEV):
        p_ref[2 + layer : 3 + layer, :] = jnp.full((1, width), h_ref[layer], jnp.float32)
    p_ref[4:8, :] = jnp.zeros((4, width), jnp.float32)
    for index, cols in enumerate(tiles(width)):
        copies[index].wait()
        moved = start[:, cols].astype(jnp.float32) + p_ref[2:3, cols] * bend(start[...], size, w_ref, p_ref, 0, cols)
        state[:, cols] = moved
        rounded[:, cols] = moved.astype(jnp.bfloat16)
    for index, cols in enumerate(tiles(width)):
        copies[len(tiles(width)) + index].wait()
        bent = bend(rounded[...], size, w_ref, p_ref, 1, cols)
        out_ref[:, cols] = (state[:, cols] + p_ref[3:4, cols] * bent).astype(jnp.bfloat16)


def total_of(parts):
    return sum(part[...].astype(jnp.float32) for part in parts)


def pass_kernel(rows, parts, keep, extra, start_ref, w_ref, p_ref, *rest):
    arrived, rest = rest[:parts], rest[parts + extra :]
    t_ref = None
    if keep:
        out_ref, t_ref, entering, state, rounded = rest
    else:
        out_ref, entering, state, rounded = rest
    size = out_ref.shape[0]
    if parts:
        came = total_of(arrived).astype(jnp.bfloat16) if parts > 1 else arrived[0][...]
        entering[:size] = jnp.where(lax.axis_index("depth") == 0, start_ref[rows, :], came)
    else:
        entering[:size] = start_ref[rows, :]
    for cols in tiles(w_ref.shape[2]):
        bent = bend(entering[...], size, w_ref, p_ref, 0, cols)
        if keep:
            t_ref[:, cols] = bent
        moved = entering[:size, cols].astype(jnp.float32) + p_ref[2:3, cols] * bent
        state[:, cols] = moved
        rounded[:size, cols] = moved.astype(jnp.bfloat16)
    for cols in tiles(w_ref.shape[2]):
        bent = bend(rounded[...], size, w_ref, p_ref, 1, cols)
        out_ref[:, cols] = (state[:, cols] + p_ref[3:4, cols] * bent).astype(jnp.bfloat16)


def relay_kernel(place, extra, came_ref, *rest):
    (out_ref,) = rest[extra:]

    @pl.when(lax.axis_index("depth") % INTERVAL == place)
    def _():
        out_ref[...] = came_ref[...]


def correction_of(entry, fresh, moved_ref):
    total = fresh - entry
    if moved_ref is not None:
        total = moved_ref[...].astype(jnp.float32) + total
    return total.astype(jnp.bfloat16)


def coarse_kernel(group, extra, parts, t_ref, w_ref, p_ref, *rest):
    (entry_parts, fresh_parts), rest = parts, rest
    entry_refs, rest = rest[:entry_parts], rest[entry_parts:]
    fresh_refs, rest = rest[:fresh_parts], rest[fresh_parts:]
    moved_ref = None
    if group > 1:
        moved_ref, before_ref, *rest = rest
    out_ref, correction_ref, rounded = rest[extra:]

    here = lax.axis_index("depth") // INTERVAL == group
    if group > 1:

        @pl.when(jnp.logical_not(here))
        def _():
            correction_ref[...] = before_ref[...]

    @pl.when(here)
    def _():
        entry = total_of(entry_refs)
        correction = correction_of(entry, total_of(fresh_refs), moved_ref)
        correction_ref[...] = correction
        size = out_ref.shape[0]
        rounded[:size] = (entry + correction.astype(jnp.float32)).astype(jnp.bfloat16)
        for cols in tiles(w_ref.shape[2]):
            bent = bend(rounded[...], size, w_ref, p_ref, 0, cols)
            change = (INTERVAL * LAY_DEV) * p_ref[2:3, cols] * (bent - t_ref[:, cols])
            out_ref[:, cols] = (correction_ref[:, cols].astype(jnp.float32) + change).astype(jnp.bfloat16)


def final_kernel(rows, groups, aliased, extra, parts, start_ref, w_ref, p_ref, moved_ref, correction_ref, *rest):
    entry_parts, fresh_parts = parts
    entry_refs, rest = rest[:entry_parts], rest[entry_parts:]
    fresh_refs, rest = rest[:fresh_parts], rest[fresh_parts + int(aliased) + extra :]
    states, token, state, first, second, sems = rest
    token[...] = jnp.zeros_like(token)
    device = lax.axis_index("depth")
    group = device // INTERVAL
    width = w_ref.shape[2]

    entry = total_of(entry_refs)

    @pl.when(group == 0)
    def _():
        state[...] = jnp.where(device == 0, start_ref[rows, :].astype(jnp.float32), entry)

    @pl.when((group > 0) & (group < groups - 1))
    def _():
        state[...] = entry + correction_ref[...].astype(jnp.float32)

    @pl.when((group > 0) & (group == groups - 1))
    def _():
        state[...] = entry + correction_of(entry, total_of(fresh_refs), moved_ref).astype(jnp.float32)

    size = state.shape[0]
    second[:size] = state[...].astype(jnp.bfloat16)
    copies = []

    def written(ref, layer, cols):
        copy = pltpu.make_async_copy(ref.at[:size, cols], states.at[layer, rows, cols], sems.at[len(copies)])
        copy.start()
        copies.append(copy)

    for cols in tiles(width):
        moved = state[:, cols] + p_ref[2:3, cols] * bend(second[...], size, w_ref, p_ref, 0, cols)
        state[:, cols] = moved
        first[:size, cols] = moved.astype(jnp.bfloat16)
        written(first, 0, cols)
    for cols in tiles(width):
        bent = bend(first[...], size, w_ref, p_ref, 1, cols)
        second[:size, cols] = (state[:, cols] + p_ref[3:4, cols] * bent).astype(jnp.bfloat16)
        written(second, 1, cols)
    for copy in copies:
        copy.wait()


def room_of(size):
    return ROWS_AT_ONCE if ROWS_AT_ONCE // 2 < size < ROWS_AT_ONCE else size


def order_of(groups):
    order, late = [], []
    for item in ORDER:
        chunk, step = divmod(item, 10)
        if step < 3:
            order.append(("pass", chunk, step))
        elif step in RELAYS:
            order.append(("relay", chunk, step))
        elif step < 5:
            if step - 2 < groups - 1:
                order.append(("coarse", chunk, step - 2))
        elif groups > 4:
            late.append(("final", chunk, 0))
        else:
            order.append(("final", chunk, 0))
    for group in range(3, groups - 1):
        order += [("coarse", chunk, group) for _, chunk, _ in late]
    return order + late


def local(initial, weights, biases, step_sizes):
    count = lax.axis_size("depth")
    groups = count // INTERVAL
    width = initial.shape[2]
    start = initial.reshape(-1, width)
    total = start.shape[0]
    bounds = [0]
    for share in SHARES:
        bounds.append(bounds[-1] + share * total // sum(SHARES))
    spans = [slice(low, high) for low, high in zip(bounds, bounds[1:])]
    sizes = [span.stop - span.start for span in spans]
    parts = len(tiles(width))
    one_on = [(source, source + 1) for source in range(count - 1)]
    ends = range(2 * INTERVAL - 1, count - 1, INTERVAL)
    straight = [pair for pair in one_on if pair[0] not in ends]

    def narrow(size):
        return kept((size, width), jnp.bfloat16)

    def call(body, outs, scratch, operands, specs=None, out_specs=None, aliases=None):
        specs = specs or [VMEM] * len(operands)
        return pl.pallas_call(
            body,
            out_shape=outs,
            in_specs=specs,
            out_specs=out_specs or jax.tree.map(lambda _: VMEM, outs),
            scratch_shapes=scratch,
            input_output_aliases=aliases or {},
            compiler_params=pltpu.CompilerParams(vmem_limit_bytes=VMEM_BYTES),
            cost_estimate=pl.CostEstimate(
                flops=2 * LAY_DEV * total * width * width, bytes_accessed=0, transcendentals=0
            ),
        )(*[held(value) if spec is VMEM else in_hbm(value) for value, spec in zip(operands, specs)])

    first = sizes[0]
    leaving, w, p = call(
        functools.partial(opening_kernel, spans[0]),
        (narrow(first), kept(weights.shape, jnp.bfloat16), kept((8, width), jnp.float32)),
        [
            pltpu.VMEM((first, width), jnp.bfloat16),
            pltpu.VMEM((first, width), jnp.float32), pltpu.VMEM((first, width), jnp.bfloat16),
            pltpu.VMEM(biases.shape, jnp.float32), pltpu.SMEM(step_sizes.shape, jnp.float32),
            DMA((LAY_DEV * parts,)), DMA((3,)),
        ],
        [start, weights, biases, step_sizes], [ANY] * 4,
    )
    chunks = len(SHARES)
    bent, correction, moved = [None] * chunks, [None] * chunks, [None] * chunks
    arrived = [[] for _ in range(chunks)]
    asides = {}
    back = {item // 10: RELAYS[item % 10] for item in ORDER if item % 10 in RELAYS}
    underway = []

    def sent(value, pairs):
        underway.append(passed_along(value, pairs))
        return underway[-1]

    def waited(values, sends):
        underway[:] = [other for other in underway if not any(other is value for value in values)]
        surplus = max(0, len(underway) + sends - UNDERWAY)
        oldest, underway[:] = underway[:surplus], underway[surplus:]
        return oldest

    def passed(value, chunk, step):
        if step == 2 and chunk in back:
            arrived[chunk].append([sent(value, straight)])
            asides[chunk] = sent(value, [(end, end - back[chunk]) for end in ends])
        elif step == 2 and chunk in APART:
            arrived[chunk].append([sent(value, straight), sent(value, [(end, end + 1) for end in ends])])
        else:
            arrived[chunk].append([sent(value, one_on)])

    passed(leaving, 0, 0)
    after, states = [leaving], None
    for kind, chunk, step in order_of(groups)[1:]:
        size = sizes[chunk]
        wide = pltpu.VMEM((size, width), jnp.float32)
        thin = pltpu.VMEM((room_of(size), width), jnp.bfloat16)
        if kind == "pass":
            keep = step == 2
            came = arrived[chunk][step - 1] if step else []
            after += waited(came, 2 if keep and (chunk in back or chunk in APART) else 1)
            result = call(
                functools.partial(pass_kernel, spans[chunk], len(came), keep, len(after)),
                (narrow(size), kept((size, width), jnp.float32)) if keep else narrow(size),
                [thin, wide, thin],
                [start, w, p] + came + after,
            )
            if keep:
                leaving, bent[chunk] = result
            else:
                leaving = result
            passed(leaving, chunk, step)
            after = [leaving]
        elif kind == "relay":
            came = [asides[chunk]]
            after += waited(came, 1)
            leaving = call(
                functools.partial(relay_kernel, INTERVAL - 1 - back[chunk], len(after)), narrow(size), [], came + after
            )
            arrived[chunk][2].append(sent(leaving, [(end - back[chunk], end + 1) for end in ends]))
            after = [leaving]
        elif kind == "coarse":
            _, entry, fresh = arrived[chunk]
            if step == 1:
                fresh = fresh[:1]
            operands = [bent[chunk], w, p] + entry + fresh
            if step > 1:
                operands += [moved[chunk], correction[chunk]]
            after += waited(operands, 1)
            delta, correction[chunk] = call(
                functools.partial(coarse_kernel, step, len(after), (len(entry), len(fresh))),
                (narrow(size), narrow(size)), [thin], operands + after,
            )
            ahead = [(source, source + INTERVAL) for source in range(step * INTERVAL, (step + 1) * INTERVAL)]
            moved[chunk] = sent(delta, ahead)
            after = [delta]
        else:
            _, entry, fresh = arrived[chunk]
            operands = [start, w, p, moved[chunk], correction[chunk]] + entry + fresh
            waited(operands, 0)
            specs = [VMEM] * len(operands)
            aliases = None
            if states is not None:
                aliases = {len(operands): 0}
                operands.append(states)
                specs.append(ANY)
            states, token = call(
                functools.partial(
                    final_kernel, spans[chunk], groups, states is not None, len(after), (len(entry), len(fresh))
                ),
                (jax.ShapeDtypeStruct((LAY_DEV, total, width), jnp.bfloat16), kept((8, 128), jnp.float32)),
                [wide, thin, thin, DMA((LAY_DEV * parts,))],
                operands + after, specs + [VMEM] * len(after), (ANY, VMEM), aliases,
            )
            after = [token]
    return states.reshape(LAY_DEV, initial.shape[0], -1, width)


def solution(mesh):
    placed = (P(), P("depth", None, None), P("depth", None), P("depth"))
    return jax.shard_map(
        local, mesh=mesh, in_specs=placed, out_specs=P("depth", None, None, None), check_vma=False
    )
```

```python
import functools

import jax
import jax.numpy as jnp
from jax import lax
from jax.experimental import pallas as pl
from jax.experimental.pallas import tpu as pltpu
from jax.sharding import PartitionSpec as P

LAY_DEV = 2
INTERVAL = 8

SHARES = (4, 5, 4, 3)
ORDER = (
    0, 20, 10, 1, 21, 11, 2, 30, 12, 3, 31, 22, 13, 17, 4, 32, 23, 14, 33, 5, 24, 34, 15, 25, 35,
)
RELAYS = {7: 2, 8: 4}
APART = ()
UNDERWAY = 5
TILE = 256
ROWS_AT_ONCE = 128
VMEM_BYTES = 20 << 20
VMEM = pl.BlockSpec(memory_space=pltpu.VMEM)
ANY = pl.BlockSpec(memory_space=pl.ANY)
DMA = pltpu.SemaphoreType.DMA


def held(value):
    return pltpu.with_memory_space_constraint(value, pltpu.VMEM)


def kept(shape, kind):
    return pltpu.VMEM(shape, kind)


def in_hbm(value):
    return pltpu.with_memory_space_constraint(value, pltpu.HBM)


def passed_along(value, pairs):
    return lax.ppermute(value, "depth", pairs)


def tiles(width):
    tile = TILE if width % TILE == 0 else width
    return [slice(low, low + tile) for low in range(0, width, tile)]


def bend(state, size, w_ref, p_ref, layer, cols):
    pre = jnp.dot(state, w_ref[layer, :, cols], preferred_element_type=jnp.float32)
    return jnp.tanh(pre[:size] + p_ref[layer : layer + 1, cols])


def opening_kernel(rows, start_hbm, w_hbm, b_hbm, h_hbm, out_ref, w_ref, p_ref, start, state, rounded, b_ref, h_ref, w_sems, sems):
    width, size = w_hbm.shape[2], out_ref.shape[0]
    small = [
        pltpu.make_async_copy(start_hbm.at[rows, :], start, sems.at[0]),
        pltpu.make_async_copy(b_hbm, b_ref, sems.at[1]),
        pltpu.make_async_copy(h_hbm, h_ref, sems.at[2]),
    ]
    for copy in small:
        copy.start()
    copies = []
    for layer in range(LAY_DEV):
        for cols in tiles(width):
            copy = pltpu.make_async_copy(
                w_hbm.at[layer, :, cols], w_ref.at[layer, :, cols], w_sems.at[len(copies)]
            )
            copy.start()
            copies.append(copy)
    for copy in small:
        copy.wait()
    p_ref[0:2, :] = b_ref[...]
    for layer in range(LAY_DEV):
        p_ref[2 + layer : 3 + layer, :] = jnp.full((1, width), h_ref[layer], jnp.float32)
    p_ref[4:8, :] = jnp.zeros((4, width), jnp.float32)
    for index, cols in enumerate(tiles(width)):
        copies[index].wait()
        moved = start[:, cols].astype(jnp.float32) + p_ref[2:3, cols] * bend(start[...], size, w_ref, p_ref, 0, cols)
        state[:, cols] = moved
        rounded[:, cols] = moved.astype(jnp.bfloat16)
    for index, cols in enumerate(tiles(width)):
        copies[len(tiles(width)) + index].wait()
        bent = bend(rounded[...], size, w_ref, p_ref, 1, cols)
        out_ref[:, cols] = (state[:, cols] + p_ref[3:4, cols] * bent).astype(jnp.bfloat16)


def total_of(parts):
    return sum(part[...].astype(jnp.float32) for part in parts)


def pass_kernel(rows, parts, keep, extra, start_ref, w_ref, p_ref, *rest):
    arrived, rest = rest[:parts], rest[parts + extra :]
    t_ref = None
    if keep:
        out_ref, t_ref, entering, state, rounded = rest
    else:
        out_ref, entering, state, rounded = rest
    size = out_ref.shape[0]
    if parts:
        came = total_of(arrived).astype(jnp.bfloat16) if parts > 1 else arrived[0][...]
        entering[:size] = jnp.where(lax.axis_index("depth") == 0, start_ref[rows, :], came)
    else:
        entering[:size] = start_ref[rows, :]
    for cols in tiles(w_ref.shape[2]):
        bent = bend(entering[...], size, w_ref, p_ref, 0, cols)
        if keep:
            t_ref[:, cols] = bent
        moved = entering[:size, cols].astype(jnp.float32) + p_ref[2:3, cols] * bent
        state[:, cols] = moved
        rounded[:size, cols] = moved.astype(jnp.bfloat16)
    for cols in tiles(w_ref.shape[2]):
        bent = bend(rounded[...], size, w_ref, p_ref, 1, cols)
        out_ref[:, cols] = (state[:, cols] + p_ref[3:4, cols] * bent).astype(jnp.bfloat16)


def relay_kernel(place, extra, came_ref, *rest):
    (out_ref,) = rest[extra:]

    @pl.when(lax.axis_index("depth") % INTERVAL == place)
    def _():
        out_ref[...] = came_ref[...]


def correction_of(entry, fresh, moved_ref):
    total = fresh - entry
    if moved_ref is not None:
        total = moved_ref[...].astype(jnp.float32) + total
    return total.astype(jnp.bfloat16)


def coarse_kernel(group, extra, parts, t_ref, w_ref, p_ref, *rest):
    (entry_parts, fresh_parts), rest = parts, rest
    entry_refs, rest = rest[:entry_parts], rest[entry_parts:]
    fresh_refs, rest = rest[:fresh_parts], rest[fresh_parts:]
    moved_ref = None
    if group > 1:
        moved_ref, before_ref, *rest = rest
    out_ref, correction_ref, rounded = rest[extra:]

    here = lax.axis_index("depth") // INTERVAL == group
    if group > 1:

        @pl.when(jnp.logical_not(here))
        def _():
            correction_ref[...] = before_ref[...]

    @pl.when(here)
    def _():
        entry = total_of(entry_refs)
        correction = correction_of(entry, total_of(fresh_refs), moved_ref)
        correction_ref[...] = correction
        size = out_ref.shape[0]
        rounded[:size] = (entry + correction.astype(jnp.float32)).astype(jnp.bfloat16)
        for cols in tiles(w_ref.shape[2]):
            bent = bend(rounded[...], size, w_ref, p_ref, 0, cols)
            change = (INTERVAL * LAY_DEV) * p_ref[2:3, cols] * (bent - t_ref[:, cols])
            out_ref[:, cols] = (correction_ref[:, cols].astype(jnp.float32) + change).astype(jnp.bfloat16)


def final_kernel(rows, groups, aliased, extra, parts, start_ref, w_ref, p_ref, moved_ref, correction_ref, *rest):
    entry_parts, fresh_parts = parts
    entry_refs, rest = rest[:entry_parts], rest[entry_parts:]
    fresh_refs, rest = rest[:fresh_parts], rest[fresh_parts + int(aliased) + extra :]
    states, token, state, first, second, sems = rest
    token[...] = jnp.zeros_like(token)
    device = lax.axis_index("depth")
    group = device // INTERVAL
    width = w_ref.shape[2]

    entry = total_of(entry_refs)

    @pl.when(group == 0)
    def _():
        state[...] = jnp.where(device == 0, start_ref[rows, :].astype(jnp.float32), entry)

    @pl.when((group > 0) & (group < groups - 1))
    def _():
        state[...] = entry + correction_ref[...].astype(jnp.float32)

    @pl.when((group > 0) & (group == groups - 1))
    def _():
        state[...] = entry + correction_of(entry, total_of(fresh_refs), moved_ref).astype(jnp.float32)

    size = state.shape[0]
    second[:size] = state[...].astype(jnp.bfloat16)
    copies = []

    def written(ref, layer, cols):
        copy = pltpu.make_async_copy(ref.at[:size, cols], states.at[layer, rows, cols], sems.at[len(copies)])
        copy.start()
        copies.append(copy)

    for cols in tiles(width):
        moved = state[:, cols] + p_ref[2:3, cols] * bend(second[...], size, w_ref, p_ref, 0, cols)
        state[:, cols] = moved
        first[:size, cols] = moved.astype(jnp.bfloat16)
        written(first, 0, cols)
    for cols in tiles(width):
        bent = bend(first[...], size, w_ref, p_ref, 1, cols)
        second[:size, cols] = (state[:, cols] + p_ref[3:4, cols] * bent).astype(jnp.bfloat16)
        written(second, 1, cols)
    for copy in copies:
        copy.wait()


def room_of(size):
    return ROWS_AT_ONCE if ROWS_AT_ONCE // 2 < size < ROWS_AT_ONCE else size


def order_of(groups):
    order, late = [], []
    for item in ORDER:
        chunk, step = divmod(item, 10)
        if step < 3:
            order.append(("pass", chunk, step))
        elif step in RELAYS:
            order.append(("relay", chunk, step))
        elif step < 5:
            if step - 2 < groups - 1:
                order.append(("coarse", chunk, step - 2))
        elif groups > 4:
            late.append(("final", chunk, 0))
        else:
            order.append(("final", chunk, 0))
    for group in range(3, groups - 1):
        order += [("coarse", chunk, group) for _, chunk, _ in late]
    return order + late


def local(initial, weights, biases, step_sizes):
    count = lax.axis_size("depth")
    groups = count // INTERVAL
    width = initial.shape[2]
    start = initial.reshape(-1, width)
    total = start.shape[0]
    bounds = [0]
    for share in SHARES:
        bounds.append(bounds[-1] + share * total // sum(SHARES))
    spans = [slice(low, high) for low, high in zip(bounds, bounds[1:])]
    sizes = [span.stop - span.start for span in spans]
    parts = len(tiles(width))
    one_on = [(source, source + 1) for source in range(count - 1)]
    ends = range(2 * INTERVAL - 1, count - 1, INTERVAL)
    straight = [pair for pair in one_on if pair[0] not in ends]

    def narrow(size):
        return kept((size, width), jnp.bfloat16)

    def call(body, outs, scratch, operands, specs=None, out_specs=None, aliases=None):
        specs = specs or [VMEM] * len(operands)
        return pl.pallas_call(
            body,
            out_shape=outs,
            in_specs=specs,
            out_specs=out_specs or jax.tree.map(lambda _: VMEM, outs),
            scratch_shapes=scratch,
            input_output_aliases=aliases or {},
            compiler_params=pltpu.CompilerParams(vmem_limit_bytes=VMEM_BYTES),
            cost_estimate=pl.CostEstimate(
                flops=2 * LAY_DEV * total * width * width, bytes_accessed=0, transcendentals=0
            ),
        )(*[held(value) if spec is VMEM else in_hbm(value) for value, spec in zip(operands, specs)])

    first = sizes[0]
    leaving, w, p = call(
        functools.partial(opening_kernel, spans[0]),
        (narrow(first), kept(weights.shape, jnp.bfloat16), kept((8, width), jnp.float32)),
        [
            pltpu.VMEM((first, width), jnp.bfloat16),
            pltpu.VMEM((first, width), jnp.float32), pltpu.VMEM((first, width), jnp.bfloat16),
            pltpu.VMEM(biases.shape, jnp.float32), pltpu.SMEM(step_sizes.shape, jnp.float32),
            DMA((LAY_DEV * parts,)), DMA((3,)),
        ],
        [start, weights, biases, step_sizes], [ANY] * 4,
    )
    chunks = len(SHARES)
    bent, correction, moved = [None] * chunks, [None] * chunks, [None] * chunks
    arrived = [[] for _ in range(chunks)]
    asides = {}
    back = {item // 10: RELAYS[item % 10] for item in ORDER if item % 10 in RELAYS}
    underway = []

    def sent(value, pairs):
        underway.append(passed_along(value, pairs))
        return underway[-1]

    def waited(values, sends):
        underway[:] = [other for other in underway if not any(other is value for value in values)]
        surplus = max(0, len(underway) + sends - UNDERWAY)
        oldest, underway[:] = underway[:surplus], underway[surplus:]
        return oldest

    def passed(value, chunk, step):
        if step == 2 and chunk in back:
            arrived[chunk].append([sent(value, straight)])
            asides[chunk] = sent(value, [(end, end - back[chunk]) for end in ends])
        elif step == 2 and chunk in APART:
            arrived[chunk].append([sent(value, straight), sent(value, [(end, end + 1) for end in ends])])
        else:
            arrived[chunk].append([sent(value, one_on)])

    passed(leaving, 0, 0)
    after, states = [leaving], None
    for kind, chunk, step in order_of(groups)[1:]:
        size = sizes[chunk]
        wide = pltpu.VMEM((size, width), jnp.float32)
        thin = pltpu.VMEM((room_of(size), width), jnp.bfloat16)
        if kind == "pass":
            keep = step == 2
            came = arrived[chunk][step - 1] if step else []
            after += waited(came, 2 if keep and (chunk in back or chunk in APART) else 1)
            result = call(
                functools.partial(pass_kernel, spans[chunk], len(came), keep, len(after)),
                (narrow(size), kept((size, width), jnp.float32)) if keep else narrow(size),
                [thin, wide, thin],
                [start, w, p] + came + after,
            )
            if keep:
                leaving, bent[chunk] = result
            else:
                leaving = result
            passed(leaving, chunk, step)
            after = [leaving]
        elif kind == "relay":
            came = [asides[chunk]]
            after += waited(came, 1)
            leaving = call(
                functools.partial(relay_kernel, INTERVAL - 1 - back[chunk], len(after)), narrow(size), [], came + after
            )
            arrived[chunk][2].append(sent(leaving, [(end - back[chunk], end + 1) for end in ends]))
            after = [leaving]
        elif kind == "coarse":
            _, entry, fresh = arrived[chunk]
            if step == 1:
                fresh = fresh[:1]
            operands = [bent[chunk], w, p] + entry + fresh
            if step > 1:
                operands += [moved[chunk], correction[chunk]]
            after += waited(operands, 1)
            delta, correction[chunk] = call(
                functools.partial(coarse_kernel, step, len(after), (len(entry), len(fresh))),
                (narrow(size), narrow(size)), [thin], operands + after,
            )
            ahead = [(source, source + INTERVAL) for source in range(step * INTERVAL, (step + 1) * INTERVAL)]
            moved[chunk] = sent(delta, ahead)
            after = [delta]
        else:
            _, entry, fresh = arrived[chunk]
            operands = [start, w, p, moved[chunk], correction[chunk]] + entry + fresh
            waited(operands, 0)
            specs = [VMEM] * len(operands)
            aliases = None
            if states is not None:
                aliases = {len(operands): 0}
                operands.append(states)
                specs.append(ANY)
            states, token = call(
                functools.partial(
                    final_kernel, spans[chunk], groups, states is not None, len(after), (len(entry), len(fresh))
                ),
                (jax.ShapeDtypeStruct((LAY_DEV, total, width), jnp.bfloat16), kept((8, 128), jnp.float32)),
                [wide, thin, thin, DMA((LAY_DEV * parts,))],
                operands + after, specs + [VMEM] * len(after), (ANY, VMEM), aliases,
            )
            after = [token]
    return states.reshape(LAY_DEV, initial.shape[0], -1, width)


def solution(mesh):
    placed = (P(), P("depth", None, None), P("depth", None), P("depth"))
    return jax.shard_map(
        local, mesh=mesh, in_specs=placed, out_specs=P("depth", None, None, None), check_vma=False
    )
```

```python
import functools

import jax
import jax.numpy as jnp
from jax import lax
from jax.experimental import pallas as pl
from jax.experimental.pallas import tpu as pltpu
from jax.sharding import PartitionSpec as P

LAY_DEV = 2
INTERVAL = 8

SHARES = (4, 5, 4, 3)
ORDER = (
    0, 20, 10, 1, 21, 11, 2, 30, 12, 3, 31, 22, 13, 17, 4, 32, 23, 14, 33, 5, 24, 34, 15, 25, 35,
)
RELAYS = {7: 2, 8: 4}
APART = ()
UNDERWAY = 5
TILE = 512
WEIGHT_TILE = 768
ROWS_AT_ONCE = 128
VMEM_BYTES = 20 << 20
VMEM = pl.BlockSpec(memory_space=pltpu.VMEM)
ANY = pl.BlockSpec(memory_space=pl.ANY)
DMA = pltpu.SemaphoreType.DMA


def held(value):
    return pltpu.with_memory_space_constraint(value, pltpu.VMEM)


def kept(shape, kind):
    return pltpu.VMEM(shape, kind)


def in_hbm(value):
    return pltpu.with_memory_space_constraint(value, pltpu.HBM)


def passed_along(value, pairs):
    return lax.ppermute(value, "depth", pairs)


def tiles(width, most=TILE):
    tile = most if width % most == 0 else width
    return [slice(low, low + tile) for low in range(0, width, tile)]


def bend(state, size, w_ref, p_ref, layer, cols):
    pre = jnp.dot(state, w_ref[layer, :, cols], preferred_element_type=jnp.float32)
    return jnp.tanh(pre[:size] + p_ref[layer : layer + 1, cols])


def opening_kernel(rows, start_hbm, w_hbm, b_hbm, h_hbm, out_ref, w_ref, p_ref, start, state, rounded, b_ref, h_ref, w_sems, sems):
    width, size = w_hbm.shape[2], out_ref.shape[0]
    small = [
        pltpu.make_async_copy(start_hbm.at[rows, :], start, sems.at[0]),
        pltpu.make_async_copy(b_hbm, b_ref, sems.at[1]),
        pltpu.make_async_copy(h_hbm, h_ref, sems.at[2]),
    ]
    for copy in small:
        copy.start()
    copies = []
    for layer in range(LAY_DEV):
        for cols in tiles(width, WEIGHT_TILE):
            copy = pltpu.make_async_copy(
                w_hbm.at[layer, :, cols], w_ref.at[layer, :, cols], w_sems.at[len(copies)]
            )
            copy.start()
            copies.append(copy)
    for copy in small:
        copy.wait()
    p_ref[0:2, :] = b_ref[...]
    for layer in range(LAY_DEV):
        p_ref[2 + layer : 3 + layer, :] = jnp.full((1, width), h_ref[layer], jnp.float32)
    p_ref[4:8, :] = jnp.zeros((4, width), jnp.float32)
    for index, cols in enumerate(tiles(width, WEIGHT_TILE)):
        copies[index].wait()
        moved = start[:, cols].astype(jnp.float32) + p_ref[2:3, cols] * bend(start[...], size, w_ref, p_ref, 0, cols)
        state[:, cols] = moved
        rounded[:, cols] = moved.astype(jnp.bfloat16)
    for index, cols in enumerate(tiles(width, WEIGHT_TILE)):
        copies[len(tiles(width, WEIGHT_TILE)) + index].wait()
        bent = bend(rounded[...], size, w_ref, p_ref, 1, cols)
        out_ref[:, cols] = (state[:, cols] + p_ref[3:4, cols] * bent).astype(jnp.bfloat16)


def total_of(parts):
    return sum(part[...].astype(jnp.float32) for part in parts)


def pass_kernel(rows, parts, keep, extra, start_ref, w_ref, p_ref, *rest):
    arrived, rest = rest[:parts], rest[parts + extra :]
    t_ref = None
    if keep:
        out_ref, t_ref, entering, state, rounded = rest
    else:
        out_ref, entering, state, rounded = rest
    size = out_ref.shape[0]
    if parts:
        came = total_of(arrived).astype(jnp.bfloat16) if parts > 1 else arrived[0][...]
        entering[:size] = jnp.where(lax.axis_index("depth") == 0, start_ref[rows, :], came)
    else:
        entering[:size] = start_ref[rows, :]
    for cols in tiles(w_ref.shape[2]):
        bent = bend(entering[...], size, w_ref, p_ref, 0, cols)
        if keep:
            t_ref[:, cols] = bent
        moved = entering[:size, cols].astype(jnp.float32) + p_ref[2:3, cols] * bent
        state[:, cols] = moved
        rounded[:size, cols] = moved.astype(jnp.bfloat16)
    for cols in tiles(w_ref.shape[2]):
        bent = bend(rounded[...], size, w_ref, p_ref, 1, cols)
        out_ref[:, cols] = (state[:, cols] + p_ref[3:4, cols] * bent).astype(jnp.bfloat16)


def relay_kernel(place, extra, came_ref, *rest):
    (out_ref,) = rest[extra:]

    @pl.when(lax.axis_index("depth") % INTERVAL == place)
    def _():
        out_ref[...] = came_ref[...]


def correction_of(entry, fresh, moved_ref):
    total = fresh - entry
    if moved_ref is not None:
        total = moved_ref[...].astype(jnp.float32) + total
    return total.astype(jnp.bfloat16)


def coarse_kernel(group, extra, parts, t_ref, w_ref, p_ref, *rest):
    (entry_parts, fresh_parts), rest = parts, rest
    entry_refs, rest = rest[:entry_parts], rest[entry_parts:]
    fresh_refs, rest = rest[:fresh_parts], rest[fresh_parts:]
    moved_ref = None
    if group > 1:
        moved_ref, before_ref, *rest = rest
    out_ref, correction_ref, rounded = rest[extra:]

    here = lax.axis_index("depth") // INTERVAL == group
    if group > 1:

        @pl.when(jnp.logical_not(here))
        def _():
            correction_ref[...] = before_ref[...]

    @pl.when(here)
    def _():
        entry = total_of(entry_refs)
        correction = correction_of(entry, total_of(fresh_refs), moved_ref)
        correction_ref[...] = correction
        size = out_ref.shape[0]
        rounded[:size] = (entry + correction.astype(jnp.float32)).astype(jnp.bfloat16)
        for cols in tiles(w_ref.shape[2]):
            bent = bend(rounded[...], size, w_ref, p_ref, 0, cols)
            change = (INTERVAL * LAY_DEV) * p_ref[2:3, cols] * (bent - t_ref[:, cols])
            out_ref[:, cols] = (correction_ref[:, cols].astype(jnp.float32) + change).astype(jnp.bfloat16)


def final_kernel(rows, groups, aliased, extra, parts, start_ref, w_ref, p_ref, moved_ref, correction_ref, *rest):
    entry_parts, fresh_parts = parts
    entry_refs, rest = rest[:entry_parts], rest[entry_parts:]
    fresh_refs, rest = rest[:fresh_parts], rest[fresh_parts + int(aliased) + extra :]
    states, token, state, first, second, sems = rest
    token[...] = jnp.zeros_like(token)
    device = lax.axis_index("depth")
    group = device // INTERVAL
    width = w_ref.shape[2]

    entry = total_of(entry_refs)

    @pl.when(group == 0)
    def _():
        state[...] = jnp.where(device == 0, start_ref[rows, :].astype(jnp.float32), entry)

    @pl.when((group > 0) & (group < groups - 1))
    def _():
        state[...] = entry + correction_ref[...].astype(jnp.float32)

    @pl.when((group > 0) & (group == groups - 1))
    def _():
        state[...] = entry + correction_of(entry, total_of(fresh_refs), moved_ref).astype(jnp.float32)

    size = state.shape[0]
    second[:size] = state[...].astype(jnp.bfloat16)
    copies = []

    def written(ref, layer, cols):
        copy = pltpu.make_async_copy(ref.at[:size, cols], states.at[layer, rows, cols], sems.at[len(copies)])
        copy.start()
        copies.append(copy)

    for cols in tiles(width):
        moved = state[:, cols] + p_ref[2:3, cols] * bend(second[...], size, w_ref, p_ref, 0, cols)
        state[:, cols] = moved
        first[:size, cols] = moved.astype(jnp.bfloat16)
        written(first, 0, cols)
    for cols in tiles(width):
        bent = bend(first[...], size, w_ref, p_ref, 1, cols)
        second[:size, cols] = (state[:, cols] + p_ref[3:4, cols] * bent).astype(jnp.bfloat16)
        written(second, 1, cols)
    for copy in copies:
        copy.wait()


def room_of(size):
    return ROWS_AT_ONCE if ROWS_AT_ONCE // 2 < size < ROWS_AT_ONCE else size


def order_of(groups):
    order, late = [], []
    for item in ORDER:
        chunk, step = divmod(item, 10)
        if step < 3:
            order.append(("pass", chunk, step))
        elif step in RELAYS:
            order.append(("relay", chunk, step))
        elif step < 5:
            if step - 2 < groups - 1:
                order.append(("coarse", chunk, step - 2))
        elif groups > 4:
            late.append(("final", chunk, 0))
        else:
            order.append(("final", chunk, 0))
    for group in range(3, groups - 1):
        order += [("coarse", chunk, group) for _, chunk, _ in late]
    return order + late


def local(initial, weights, biases, step_sizes):
    count = lax.axis_size("depth")
    groups = count // INTERVAL
    width = initial.shape[2]
    start = initial.reshape(-1, width)
    total = start.shape[0]
    bounds = [0]
    for share in SHARES:
        bounds.append(bounds[-1] + share * total // sum(SHARES))
    spans = [slice(low, high) for low, high in zip(bounds, bounds[1:])]
    sizes = [span.stop - span.start for span in spans]
    parts = len(tiles(width))
    one_on = [(source, source + 1) for source in range(count - 1)]
    ends = range(2 * INTERVAL - 1, count - 1, INTERVAL)
    straight = [pair for pair in one_on if pair[0] not in ends]

    def narrow(size):
        return kept((size, width), jnp.bfloat16)

    def call(body, outs, scratch, operands, specs=None, out_specs=None, aliases=None):
        specs = specs or [VMEM] * len(operands)
        return pl.pallas_call(
            body,
            out_shape=outs,
            in_specs=specs,
            out_specs=out_specs or jax.tree.map(lambda _: VMEM, outs),
            scratch_shapes=scratch,
            input_output_aliases=aliases or {},
            compiler_params=pltpu.CompilerParams(vmem_limit_bytes=VMEM_BYTES),
            cost_estimate=pl.CostEstimate(
                flops=2 * LAY_DEV * total * width * width, bytes_accessed=0, transcendentals=0
            ),
        )(*[held(value) if spec is VMEM else in_hbm(value) for value, spec in zip(operands, specs)])

    first = sizes[0]
    leaving, w, p = call(
        functools.partial(opening_kernel, spans[0]),
        (narrow(first), kept(weights.shape, jnp.bfloat16), kept((8, width), jnp.float32)),
        [
            pltpu.VMEM((first, width), jnp.bfloat16),
            pltpu.VMEM((first, width), jnp.float32), pltpu.VMEM((first, width), jnp.bfloat16),
            pltpu.VMEM(biases.shape, jnp.float32), pltpu.SMEM(step_sizes.shape, jnp.float32),
            DMA((LAY_DEV * parts,)), DMA((3,)),
        ],
        [start, weights, biases, step_sizes], [ANY] * 4,
    )
    chunks = len(SHARES)
    bent, correction, moved = [None] * chunks, [None] * chunks, [None] * chunks
    arrived = [[] for _ in range(chunks)]
    asides = {}
    back = {item // 10: RELAYS[item % 10] for item in ORDER if item % 10 in RELAYS}
    underway = []

    def sent(value, pairs):
        underway.append(passed_along(value, pairs))
        return underway[-1]

    def waited(values, sends):
        underway[:] = [other for other in underway if not any(other is value for value in values)]
        surplus = max(0, len(underway) + sends - UNDERWAY)
        oldest, underway[:] = underway[:surplus], underway[surplus:]
        return oldest

    def passed(value, chunk, step):
        if step == 2 and chunk in back:
            arrived[chunk].append([sent(value, straight)])
            asides[chunk] = sent(value, [(end, end - back[chunk]) for end in ends])
        elif step == 2 and chunk in APART:
            arrived[chunk].append([sent(value, straight), sent(value, [(end, end + 1) for end in ends])])
        else:
            arrived[chunk].append([sent(value, one_on)])

    passed(leaving, 0, 0)
    after, states = [leaving], None
    for kind, chunk, step in order_of(groups)[1:]:
        size = sizes[chunk]
        wide = pltpu.VMEM((size, width), jnp.float32)
        thin = pltpu.VMEM((room_of(size), width), jnp.bfloat16)
        if kind == "pass":
            keep = step == 2
            came = arrived[chunk][step - 1] if step else []
            after += waited(came, 2 if keep and (chunk in back or chunk in APART) else 1)
            result = call(
                functools.partial(pass_kernel, spans[chunk], len(came), keep, len(after)),
                (narrow(size), kept((size, width), jnp.float32)) if keep else narrow(size),
                [thin, wide, thin],
                [start, w, p] + came + after,
            )
            if keep:
                leaving, bent[chunk] = result
            else:
                leaving = result
            passed(leaving, chunk, step)
            after = [leaving]
        elif kind == "relay":
            came = [asides[chunk]]
            after += waited(came, 1)
            leaving = call(
                functools.partial(relay_kernel, INTERVAL - 1 - back[chunk], len(after)), narrow(size), [], came + after
            )
            arrived[chunk][2].append(sent(leaving, [(end - back[chunk], end + 1) for end in ends]))
            after = [leaving]
        elif kind == "coarse":
            _, entry, fresh = arrived[chunk]
            if step == 1:
                fresh = fresh[:1]
            operands = [bent[chunk], w, p] + entry + fresh
            if step > 1:
                operands += [moved[chunk], correction[chunk]]
            after += waited(operands, 1)
            delta, correction[chunk] = call(
                functools.partial(coarse_kernel, step, len(after), (len(entry), len(fresh))),
                (narrow(size), narrow(size)), [thin], operands + after,
            )
            ahead = [(source, source + INTERVAL) for source in range(step * INTERVAL, (step + 1) * INTERVAL)]
            moved[chunk] = sent(delta, ahead)
            after = [delta]
        else:
            _, entry, fresh = arrived[chunk]
            operands = [start, w, p, moved[chunk], correction[chunk]] + entry + fresh
            waited(operands, 0)
            specs = [VMEM] * len(operands)
            aliases = None
            if states is not None:
                aliases = {len(operands): 0}
                operands.append(states)
                specs.append(ANY)
            states, token = call(
                functools.partial(
                    final_kernel, spans[chunk], groups, states is not None, len(after), (len(entry), len(fresh))
                ),
                (jax.ShapeDtypeStruct((LAY_DEV, total, width), jnp.bfloat16), kept((8, 128), jnp.float32)),
                [wide, thin, thin, DMA((LAY_DEV * parts,))],
                operands + after, specs + [VMEM] * len(after), (ANY, VMEM), aliases,
            )
            after = [token]
    return states.reshape(LAY_DEV, initial.shape[0], -1, width)


def solution(mesh):
    placed = (P(), P("depth", None, None), P("depth", None), P("depth"))
    return jax.shard_map(
        local, mesh=mesh, in_specs=placed, out_specs=P("depth", None, None, None), check_vma=False
    )
```
